768 devices in a mesh: fsdp: 64 (over x, y, core), own: 12 (over z).
Axes of the slice: x: 4, y: 8, z: 12, core: 2. Of those that a mesh axis runs over, the one named last changes fastest.
Arguments:
- grads: bfloat16 [64, 24, 288, 1024], P('fsdp', 'own'), may hold values from -5 to 5
- momentum: float32 [24, 288, 1024], P('own', None, 'fsdp'), may hold values from -6 to 6
- weights: float32 [24, 288, 1024], P('own', None, 'fsdp'), may hold values from -6 to 6
- live_rows: int32 [24], replicated, may hold values from 144 to 288, as said below
Outputs:
- new_momentum: float32 [24, 288, 1024], P('own', None, 'fsdp')
- update: float32 [24, 288, 1024], P('own', None, 'fsdp')
The draws below stay inside these ranges and needn't reach their ends.
Inputs may be any that keep to these rules, and one draw needn't show every extreme that they name: live_rows[j] is the number of real rows of matrix j; both bounds are reached in every draw.
All inputs are finite; a program needn't handle non-finite values.
Results may differ from the reference program's by a relative error of at most 0.019.
Values may be sent and summed in bfloat16 or wider, within the bound.
No kernel may reach another device: no remote copies, remote signals or barrier semaphores. Data moves between devices by JAX's collectives and lax.ppermute only.
A program may use at most 32 MiB of HBM per device.

```python
import math
import jax
import jax.numpy as jnp
from jax import lax

COLS = 1024
ROWS = 288
ITERS = 5
NMAT = 24
N_FSDP = 64


def draw_live_rows(key, part):
    key = jax.random.fold_in(key, 7)
    first_key, second_key, third_key = jax.random.split(key, 3)
    values = jax.random.randint(first_key, (NMAT,), ROWS // 2, ROWS + 1)
    top_place = jax.random.randint(second_key, (), 0, NMAT)
    offset = jax.random.randint(third_key, (), 1, NMAT)
    low_place = (top_place + offset) % NMAT
    indices = jnp.arange(NMAT)
    values = jnp.where(indices == top_place, ROWS, values)
    values = jnp.where(indices == low_place, ROWS // 2, values)
    return values.astype(jnp.int32)


def spiked(array, key, source, target, blocks, factor):
    def block_of(axis_at):
        return (jnp.arange(array.shape[axis_at]) // (array.shape[axis_at] // blocks)).reshape((-1,) + (1,) * (array.ndim - 1 - axis_at))

    near = jax.random.permutation(key, blocks)[block_of(target)]
    far = (block_of(target) + blocks // 2) % blocks
    return jnp.where((block_of(source) == near) | (block_of(source) == far), factor * array, array)


def levels(stream_key, dims, cuts, smallest, high):
    gain, own = 1.0, jax.random.fold_in(stream_key, 6)
    for position, parts in cuts:
        draws = jnp.exp(jax.random.uniform(jax.random.fold_in(own, position), (parts,), jnp.float32, smallest / len(cuts), high / len(cuts)))
        gain = gain * jnp.repeat(draws, dims[position] // parts).reshape([-1 if axis == position else 1 for axis in range(len(dims))])
    return gain


def normal_values(stream_key, extent, scale, most, cuts=(), kind=jnp.bfloat16):
    level = levels(stream_key, extent, cuts, -0.22, 0.18) if cuts else 1.0
    drawn = jax.random.normal(stream_key, extent, jnp.float32) * scale * level
    return jnp.minimum(jnp.maximum(drawn, -most), most).astype(kind)


def bell_draw_with(key, extent, width, most, cuts, heavy, kind=jnp.bfloat16):
    result = width * jax.random.normal(key, extent, jnp.float32)
    if cuts:
        result = result * levels(key, extent, cuts, -0.22, 0.18)
    return jnp.clip(spiked(result, jax.random.fold_in(key, 3), *heavy), -most, most).astype(kind)


def setup_inputs(seed: int = 0) -> dict:
    splits = jax.random.split(jax.random.key(seed), 5)
    return {
        "grads": bell_draw_with(splits[0], (N_FSDP, NMAT, ROWS, COLS), 0.125, 5.0, ((0, 64), (1, 12)), (0, 3, 64, 4.0)),
        "momentum": normal_values(splits[1], (NMAT, ROWS, COLS), 1.0, 6.0, ((0, 12), (2, 64)), jnp.float32),
        "weights": normal_values(splits[2], (NMAT, ROWS, COLS), 1.0, 6.0, ((0, 12), (2, 64)), jnp.float32),
        "live_rows": draw_live_rows(jax.random.fold_in(splits[4], 71), 0),
    }


MOMENTUM_DECAY = 0.95
NORM_EPS = 1e-07
NEWTON_FIRST = 3.4445
NEWTON_SECOND = -4.775
NEWTON_THIRD = 2.0315
UPDATE_SCALE = 0.2
WEIGHT_DECAY = 0.1

def newton_schulz(matrix):
    for _ in range(ITERS):
        gram_block = jnp.dot(matrix, matrix.T, preferred_element_type=jnp.float32).astype(jnp.bfloat16)
        square = jnp.dot(gram_block, gram_block, preferred_element_type=jnp.float32)
        poly_block = (NEWTON_SECOND * gram_block.astype(jnp.float32) + NEWTON_THIRD * square).astype(jnp.bfloat16)
        product = jnp.dot(poly_block, matrix, preferred_element_type=jnp.float32)
        matrix = (NEWTON_FIRST * matrix.astype(jnp.float32) + product).astype(jnp.bfloat16)
    return matrix

def reference(grads, momentum, weights, live_rows):

    def add_replica(step_index, total_sum):
        return total_sum + grads[step_index].astype(jnp.float32)
    summed = lax.fori_loop(0, grads.shape[0], add_replica, jnp.zeros(grads.shape[1:], jnp.float32))
    row_ids = jnp.arange(ROWS, dtype=jnp.int32)
    row_mask = (row_ids[None, :, None] < live_rows[:, None, None]).astype(jnp.float32)
    new_momentum = (MOMENTUM_DECAY * momentum + summed) * row_mask
    norm_values = jnp.sqrt(lax.optimization_barrier(jnp.sum(new_momentum * new_momentum, axis=(1, 2))))
    start_block = (new_momentum / (norm_values[:, None, None] + NORM_EPS)).astype(jnp.bfloat16)
    ortho = lax.map(newton_schulz, start_block)
    update = UPDATE_SCALE * math.sqrt(COLS) * ortho.astype(jnp.float32) + WEIGHT_DECAY * weights
    return (new_momentum, update)
```

```python
import functools
import math

import jax
import jax.numpy as jnp
from jax import lax
from jax.experimental import pallas as pl
from jax.experimental.pallas import tpu as pltpu
from jax.sharding import Mesh, PartitionSpec as P

ITERS = 5
MOMENTUM_DECAY = 0.95
NORM_EPS = 1e-07
NEWTON_FIRST = 3.4445
NEWTON_SECOND = -4.775
NEWTON_THIRD = 2.0315
UPDATE_SCALE = 0.2
WEIGHT_DECAY = 0.1

SMEM = pl.BlockSpec(memory_space=pltpu.SMEM)
VMEM = pl.BlockSpec(memory_space=pltpu.VMEM)
VMEM_LIMIT = 32 * 1024 * 1024
NT = (((1,), (1,)), ((), ()))
NN = (((1,), (0,)), ((), ()))


def mm(a, b, dims):
    return lax.dot_general(a, b, dims, preferred_element_type=jnp.float32)


def pair_sum_kernel(both_ref, out_ref):
    total = both_ref[0].astype(jnp.float32) + both_ref[1].astype(jnp.float32)
    out_ref[...] = total.astype(jnp.bfloat16).T.reshape(out_ref.shape)


def pair_sum(both, chips, cols):
    height, width = both.shape[1:]
    steps = 4
    return pl.pallas_call(
        pair_sum_kernel,
        grid=(steps,),
        in_specs=[pl.BlockSpec((2, height, width // steps), lambda i: (0, 0, i))],
        out_specs=pl.BlockSpec((chips // steps, cols, height), lambda i: (i, 0, 0)),
        out_shape=jax.ShapeDtypeStruct((chips, cols, height), jnp.bfloat16),
        compiler_params=pltpu.CompilerParams(vmem_limit_bytes=VMEM_LIMIT),
    )(both)


def momentum_kernel(place_ref, live_ref, parts_ref, old_ref, new_ref, copies_ref):
    chips = parts_ref.shape[0]
    summed = parts_ref[0].astype(jnp.float32)
    for k in range(1, chips):
        summed = summed + parts_ref[k].astype(jnp.float32)
    rows = lax.broadcasted_iota(jnp.int32, summed.shape, 1)
    live = live_ref[place_ref[0]]
    new = jnp.where(rows < live, MOMENTUM_DECAY * old_ref[...] + summed, 0.0)
    new_ref[...] = new
    rounded = new.astype(jnp.bfloat16)
    for k in range(chips):
        copies_ref[k] = rounded


def momentum_step(place, live_rows, parts, old):
    return pl.pallas_call(
        momentum_kernel,
        in_specs=[SMEM, SMEM, VMEM, VMEM],
        out_specs=[VMEM, VMEM],
        out_shape=[
            jax.ShapeDtypeStruct(old.shape, jnp.float32),
            jax.ShapeDtypeStruct(parts.shape, jnp.bfloat16),
        ],
        compiler_params=pltpu.CompilerParams(vmem_limit_bytes=VMEM_LIMIT),
    )(place, live_rows, parts, old)


def newton_kernel(place_ref, gathered_ref, out_ref):
    chips, cols, height = gathered_ref.shape
    width = chips * cols
    x = gathered_ref[...].reshape(width, height).T
    raw = mm(x, x, NT)
    row = lax.broadcasted_iota(jnp.int32, (height, height), 0)
    col = lax.broadcasted_iota(jnp.int32, (height, height), 1)
    norm = jnp.sqrt(jnp.sum(jnp.where(row == col, raw, 0.0), keepdims=True))
    scale = 1.0 / (norm + NORM_EPS)
    gram = (raw * scale * scale).astype(jnp.bfloat16)
    for step in range(ITERS):
        if step:
            gram = mm(x, x, NT).astype(jnp.bfloat16)
        square = mm(gram, gram, NN)
        poly = (NEWTON_SECOND * gram.astype(jnp.float32) + NEWTON_THIRD * square).astype(jnp.bfloat16)
        if step == ITERS - 1:
            place = place_ref[1] * cols
            want = lax.broadcasted_iota(jnp.int32, (cols, width), 0) + place
            have = lax.broadcasted_iota(jnp.int32, (cols, width), 1)
            pick = (want == have).astype(jnp.bfloat16)
            mine = mm(pick, x, NT)
            out_ref[...] = NEWTON_FIRST * mine + mm(mine.astype(jnp.bfloat16), poly, NT)
        else:
            x = NEWTON_FIRST * x.astype(jnp.float32) + mm(poly, x, NN)
            if step == 0:
                x = x * scale
            x = x.astype(jnp.bfloat16)


def newton(place, gathered):
    return pl.pallas_call(
        newton_kernel,
        in_specs=[SMEM, VMEM],
        out_specs=VMEM,
        out_shape=jax.ShapeDtypeStruct(gathered.shape[1:], jnp.float32),
        compiler_params=pltpu.CompilerParams(vmem_limit_bytes=VMEM_LIMIT),
    )(place, gathered)


def per_device(grads, momentum, weights, live_rows):
    cores = lax.axis_size("core")
    chips = lax.axis_size("x") * lax.axis_size("y")
    slab = momentum.shape[2]
    height = momentum.shape[1]
    cols = cores * slab
    width = chips * cols
    chip = lax.axis_index("x") * lax.axis_size("y") + lax.axis_index("y")
    matrix = lax.axis_index("own") * cores + lax.axis_index("core")
    place = jnp.stack([matrix, chip]).astype(jnp.int32)
    both = lax.all_to_all(grads[0], "core", 0, 0)
    old = lax.all_to_all(jnp.swapaxes(momentum, 1, 2), "core", 0, 0)
    parts = pair_sum(both, chips, cols)
    parts = lax.all_to_all(parts, ("x", "y"), 0, 0)
    new, copies = momentum_step(place, live_rows, parts, old.reshape(cols, height))
    gathered = lax.all_to_all(copies, ("x", "y"), 0, 0)
    ortho = newton(place, gathered)
    back = jnp.stack([new.reshape(cores, slab, height), ortho.reshape(cores, slab, height)], axis=1)
    back = lax.all_to_all(back, "core", 0, 0)
    new_momentum = jnp.swapaxes(back[:, 0], 1, 2)
    update = UPDATE_SCALE * math.sqrt(width) * jnp.swapaxes(back[:, 1], 1, 2) + WEIGHT_DECAY * weights
    return (new_momentum, update)


def solution(mesh):
    fsdp, own = mesh.devices.shape
    assert (fsdp, own) == (64, 12)
    split = Mesh(mesh.devices.reshape(4, 8, 2, own), ("x", "y", "core", "own"))
    all_fsdp = ("x", "y", "core")
    in_specs = (P(all_fsdp, "own", None, None), P("own", None, all_fsdp), P("own", None, all_fsdp), P())
    out_specs = (P("own", None, all_fsdp), P("own", None, all_fsdp))
    return jax.shard_map(
        per_device, mesh=split, in_specs=in_specs, out_specs=out_specs, check_vma=False
    )
```

```python
import math

import jax
import jax.numpy as jnp
from jax import lax
from jax.experimental import pallas as pl
from jax.experimental.pallas import tpu as pltpu
from jax.sharding import Mesh, PartitionSpec as P

ITERS = 5
MOMENTUM_DECAY = 0.95
NORM_EPS = 1e-07
NEWTON_FIRST = 3.4445
NEWTON_SECOND = -4.775
NEWTON_THIRD = 2.0315
UPDATE_SCALE = 0.2
WEIGHT_DECAY = 0.1

LANES = 128
SMEM = pl.BlockSpec(memory_space=pltpu.SMEM)
VMEM = pl.BlockSpec(memory_space=pltpu.VMEM)
PARAMS = pltpu.CompilerParams(vmem_limit_bytes=32 * 1024 * 1024)
NT = (((1,), (1,)), ((), ()))
NN = (((1,), (0,)), ((), ()))
TN = (((0,), (0,)), ((), ()))

CORE, CHIP, MATRIX = 0, 1, 2


def mm(a, b, dims, precision=None):
    return lax.dot_general(a, b, dims, precision=precision, preferred_element_type=jnp.float32)


def pair_sum_kernel(place_ref, own_ref, other_ref, old_ref, out_ref):
    step = pl.program_id(0)
    chunks = out_ref.shape[0]
    total = own_ref[0].astype(jnp.float32) + other_ref[...].astype(jnp.float32)
    for q in range(chunks):
        out_ref[q] = total[:, q * LANES:(q + 1) * LANES].astype(jnp.bfloat16)
    cores, _, slab, height = old_ref.shape
    cols = cores * slab
    per_chunk = LANES // cols
    chip = place_ref[CHIP]

    @pl.when(chip // per_chunk // chunks == step)
    def _():
        old = MOMENTUM_DECAY * old_ref[:, 0].reshape(cols, height)
        want = lax.broadcasted_iota(jnp.int32, (cols, LANES), 0) + (chip % per_chunk) * cols
        have = lax.broadcasted_iota(jnp.int32, (cols, LANES), 1)
        spread = mm(old, (want == have).astype(jnp.float32), TN, lax.Precision.HIGHEST)
        for q in range(chunks):

            @pl.when(chip // per_chunk % chunks == q)
            def _():
                mine = total[:, q * LANES:(q + 1) * LANES] + spread
                out_ref[q] = mine.astype(jnp.bfloat16)


def pair_sum(place, own, other, old):
    height, width = other.shape
    cores, _, slab, _ = old.shape
    steps = 2
    chunks = width // LANES // steps
    return pl.pallas_call(
        pair_sum_kernel,
        grid_spec=pltpu.PrefetchScalarGridSpec(
            num_scalar_prefetch=1,
            grid=(steps,),
            in_specs=[
                pl.BlockSpec((1, height, chunks * LANES), lambda i, place: (place[CORE], 0, i)),
                pl.BlockSpec((height, chunks * LANES), lambda i, place: (0, i)),
                pl.BlockSpec((cores, 1, slab, height), lambda i, place: (0, place[CORE], 0, 0)),
            ],
            out_specs=pl.BlockSpec((chunks, height, LANES), lambda i, place: (i, 0, 0)),
        ),
        out_shape=jax.ShapeDtypeStruct((width // LANES, height, LANES), jnp.bfloat16),
        compiler_params=PARAMS,
    )(place, own, other, old)


def add_parts(parts_ref):
    total = parts_ref[0].astype(jnp.float32)
    for k in range(1, parts_ref.shape[0]):
        total = total + parts_ref[k].astype(jnp.float32)
    return total


def sum_kernel(parts_ref, copies_ref):
    total = add_parts(parts_ref).astype(jnp.bfloat16)
    for k in range(copies_ref.shape[0]):
        copies_ref[k] = total


def sum_and_copy(parts, copies):
    return pl.pallas_call(
        sum_kernel,
        in_specs=[VMEM],
        out_specs=VMEM,
        out_shape=jax.ShapeDtypeStruct((copies,) + parts.shape[1:], jnp.bfloat16),
        compiler_params=PARAMS,
    )(parts)


def mask_kernel(place_ref, live_ref, parts_ref, copies_ref):
    total = add_parts(parts_ref)
    rows = lax.broadcasted_iota(jnp.int32, total.shape, 0)
    live = live_ref[place_ref[MATRIX]]
    new = jnp.where(rows < live, total, 0.0).astype(jnp.bfloat16)
    for k in range(copies_ref.shape[0]):
        copies_ref[k] = new


def sum_mask_and_copy(place, live_rows, parts, copies):
    return pl.pallas_call(
        mask_kernel,
        in_specs=[SMEM, SMEM, VMEM],
        out_specs=VMEM,
        out_shape=jax.ShapeDtypeStruct((copies,) + parts.shape[1:], jnp.bfloat16),
        compiler_params=PARAMS,
    )(place, live_rows, parts)


def newton_kernel(place_ref, gathered_ref, out_ref):
    chunks, height, _ = gathered_ref.shape
    cols = out_ref.shape[1]
    width = chunks * LANES
    x = jnp.concatenate([gathered_ref[q] for q in range(chunks)], axis=1)
    want = lax.broadcasted_iota(jnp.int32, (cols, width), 0) + place_ref[CHIP] * cols
    have = lax.broadcasted_iota(jnp.int32, (cols, width), 1)
    pick = (want == have).astype(jnp.bfloat16)
    out_ref[0] = mm(pick, x, NT)
    raw = mm(x, x, NT)
    row = lax.broadcasted_iota(jnp.int32, (height, height), 0)
    col = lax.broadcasted_iota(jnp.int32, (height, height), 1)
    norm = jnp.sqrt(jnp.sum(jnp.where(row == col, raw, 0.0), keepdims=True))
    scale = 1.0 / (norm + NORM_EPS)
    gram = (raw * scale * scale).astype(jnp.bfloat16)
    for step in range(ITERS):
        if step:
            gram = mm(x, x, NT).astype(jnp.bfloat16)
        square = mm(gram, gram, NN)
        poly = (NEWTON_SECOND * gram.astype(jnp.float32) + NEWTON_THIRD * square).astype(jnp.bfloat16)
        if step == ITERS - 1:
            mine = mm(pick, x, NT)
            out_ref[1] = NEWTON_FIRST * mine + mm(mine.astype(jnp.bfloat16), poly, NT)
        else:
            x = NEWTON_FIRST * x.astype(jnp.float32) + mm(poly, x, NN)
            if step == 0:
                x = x * scale
            x = x.astype(jnp.bfloat16)


def newton(place, gathered, cols):
    return pl.pallas_call(
        newton_kernel,
        in_specs=[SMEM, VMEM],
        out_specs=VMEM,
        out_shape=jax.ShapeDtypeStruct((2, cols, gathered.shape[1]), jnp.float32),
        compiler_params=PARAMS,
    )(place, gathered)


def finish_kernel(factor, place_ref, back_ref, weights_ref, new_ref, update_ref):
    mats, slab, _ = weights_ref.shape
    mine = pl.ds(pl.multiple_of(place_ref[CORE] * slab, slab), slab)
    for m in range(mats):
        new_ref[m] = back_ref[m, 0, mine, :]
        update_ref[m] = factor * back_ref[m, 1, mine, :] + WEIGHT_DECAY * weights_ref[m]


def finish(place, back, weights, factor):
    def kernel(*refs):
        finish_kernel(factor, *refs)

    shape = jax.ShapeDtypeStruct(weights.shape, jnp.float32)
    return pl.pallas_call(
        kernel,
        in_specs=[SMEM, VMEM, VMEM],
        out_specs=[VMEM, VMEM],
        out_shape=[shape, shape],
        compiler_params=PARAMS,
    )(place, back, weights)


def per_device(grads, momentum, weights, live_rows):
    mats, height, slab = momentum.shape
    cores = lax.axis_size("core")
    y_low, y_high = lax.axis_size("y_low"), lax.axis_size("y_high")
    width = grads.shape[3]
    core = lax.axis_index("core")
    chip = (lax.axis_index("x") * y_high + lax.axis_index("y_high")) * y_low + lax.axis_index("y_low")
    matrix = lax.axis_index("own") * mats + core
    place = jnp.stack([core, chip, matrix]).astype(jnp.int32)
    group = ("x", "y_low")
    given = lax.dynamic_index_in_dim(grads[0], cores - 1 - core, 0, keepdims=False)
    other = lax.ppermute(given, "core", [(0, 1), (1, 0)])
    old = lax.all_gather(jnp.swapaxes(momentum, 1, 2), "core")
    chunks = pair_sum(place, grads[0], other, old)
    chunks = lax.all_to_all(chunks, group, 0, 0)
    chunk = sum_and_copy(chunks, y_high)
    chunk = lax.all_to_all(chunk, "y_high", 0, 0)
    copies = sum_mask_and_copy(place, live_rows, chunk, width // LANES)
    gathered = lax.all_to_all(copies, group, 0, 0)
    mine = newton(place, gathered, cores * slab)
    back = lax.all_gather(mine, "core")
    new_momentum, update = finish(
        place, back, jnp.swapaxes(weights, 1, 2), UPDATE_SCALE * math.sqrt(width)
    )
    return (jnp.swapaxes(new_momentum, 1, 2), jnp.swapaxes(update, 1, 2))


def solution(mesh):
    fsdp, own = mesh.devices.shape
    assert (fsdp, own) == (64, 12)
    split = Mesh(mesh.devices.reshape(4, 4, 2, 2, own), ("x", "y_high", "y_low", "core", "own"))
    all_fsdp = ("x", "y_high", "y_low", "core")
    in_specs = (P(all_fsdp, "own", None, None), P("own", None, all_fsdp), P("own", None, all_fsdp), P())
    out_specs = (P("own", None, all_fsdp), P("own", None, all_fsdp))
    return jax.shard_map(
        per_device, mesh=split, in_specs=in_specs, out_specs=out_specs, check_vma=False
    )
```

```python
import functools
import math

import jax
import jax.numpy as jnp
from jax import lax
from jax.experimental import pallas as pl
from jax.experimental.pallas import tpu as pltpu
from jax.sharding import Mesh, PartitionSpec as P

ITERS = 5
MOMENTUM_DECAY = 0.95
NORM_EPS = 1e-07
NEWTON_FIRST = 3.4445
NEWTON_SECOND = -4.775
NEWTON_THIRD = 2.0315
UPDATE_SCALE = 0.2
WEIGHT_DECAY = 0.1

LANES = 128
VMEM = pl.BlockSpec(memory_space=pltpu.VMEM)
PARAMS = pltpu.CompilerParams(vmem_limit_bytes=32 * 1024 * 1024)
NT = (((1,), (1,)), ((), ()))
NN = (((1,), (0,)), ((), ()))
TN = (((0,), (0,)), ((), ()))

def chip_index():
    y = lax.axis_index("y_high") * lax.axis_size("y_low") + lax.axis_index("y_low")
    return lax.axis_index("x") * (lax.axis_size("y_high") * lax.axis_size("y_low")) + y


def mm(a, b, dims, precision=None):
    return lax.dot_general(a, b, dims, precision=precision, preferred_element_type=jnp.float32)


def pair_sum_kernel(own_ref, other_ref, old_ref, out_ref):
    core, chip = lax.axis_index("core"), chip_index()
    for q in range(out_ref.shape[0]):
        lanes = slice(q * LANES, (q + 1) * LANES)
        total = own_ref[core, :, lanes].astype(jnp.float32) + other_ref[:, lanes].astype(jnp.float32)
        out_ref[q] = total.astype(jnp.bfloat16)
    cores, _, slab, height = old_ref.shape
    cols = cores * slab
    per_chunk = LANES // cols
    chunk, slot = chip // per_chunk, chip % per_chunk
    old = jnp.concatenate([old_ref[k, core] for k in range(cores)], axis=0)
    want = lax.broadcasted_iota(jnp.int32, (cols, LANES), 0) + slot * cols
    have = lax.broadcasted_iota(jnp.int32, (cols, LANES), 1)
    pick = (want == have).astype(jnp.float32)
    spread = mm(MOMENTUM_DECAY * old, pick, TN, lax.Precision.HIGHEST)
    lanes = pl.ds(pl.multiple_of(chunk * LANES, LANES), LANES)
    total = own_ref[core, :, lanes].astype(jnp.float32) + other_ref[:, lanes].astype(jnp.float32)
    out_ref[chunk] = (total + spread).astype(jnp.bfloat16)


def pair_sum(own, other, old):
    height, width = other.shape
    return pl.pallas_call(
        pair_sum_kernel,
        in_specs=[VMEM, VMEM, VMEM],
        out_specs=VMEM,
        out_shape=jax.ShapeDtypeStruct((width // LANES, height, LANES), jnp.bfloat16),
        compiler_params=PARAMS,
    )(own, other, old)


def add_parts(parts_ref):
    total = parts_ref[0].astype(jnp.float32)
    for k in range(1, parts_ref.shape[0]):
        total = total + parts_ref[k].astype(jnp.float32)
    return total


def sum_kernel(parts_ref, copies_ref):
    total = add_parts(parts_ref).astype(jnp.bfloat16)
    for k in range(copies_ref.shape[0]):
        copies_ref[k] = total


def sum_and_copy(parts, copies):
    return pl.pallas_call(
        sum_kernel,
        in_specs=[VMEM],
        out_specs=VMEM,
        out_shape=jax.ShapeDtypeStruct((copies,) + parts.shape[1:], jnp.bfloat16),
        compiler_params=PARAMS,
    )(parts)


def mask_kernel(mats, live_ref, parts_ref, copies_ref):
    total = add_parts(parts_ref)
    rows = lax.broadcasted_iota(jnp.int32, total.shape, 0)
    matrix = lax.axis_index("own") * mats + lax.axis_index("core")
    which = lax.broadcasted_iota(jnp.int32, live_ref.shape, 1) == matrix
    live = jnp.sum(jnp.where(which, live_ref[...], 0), axis=1, keepdims=True)
    new = jnp.where(rows < live, total, 0.0).astype(jnp.bfloat16)
    for k in range(copies_ref.shape[0]):
        copies_ref[k] = new


def sum_mask_and_copy(mats, live_rows, parts, copies):
    return pl.pallas_call(
        functools.partial(mask_kernel, mats),
        in_specs=[VMEM, VMEM],
        out_specs=VMEM,
        out_shape=jax.ShapeDtypeStruct((copies,) + parts.shape[1:], jnp.bfloat16),
        compiler_params=PARAMS,
    )(live_rows[None, :], parts)


def newton_kernel(gathered_ref, out_ref, x_ref):
    chunks, height, _ = gathered_ref.shape
    cols = out_ref.shape[1]
    per_chunk = LANES // cols
    chunk, slot = chip_index() // per_chunk, chip_index() % per_chunk
    want = lax.broadcasted_iota(jnp.int32, (cols, LANES), 0) + slot * cols
    have = lax.broadcasted_iota(jnp.int32, (cols, LANES), 1)
    pick = (want == have).astype(jnp.bfloat16)
    out_ref[0] = mm(pick, gathered_ref[chunk], NT)
    row = lax.broadcasted_iota(jnp.int32, (height, height), 0)
    col = lax.broadcasted_iota(jnp.int32, (height, height), 1)
    source = gathered_ref
    for step in range(ITERS):
        x = jnp.concatenate([source[q] for q in range(chunks)], axis=1)
        gram = mm(x, x, NT)
        if step == 0:
            norm = jnp.sqrt(jnp.sum(jnp.where(row == col, gram, 0.0), keepdims=True))
            scale = 1.0 / (norm + NORM_EPS)
            gram = gram * scale * scale
        gram = gram.astype(jnp.bfloat16)
        square = mm(gram, gram, NN)
        poly = (NEWTON_SECOND * gram.astype(jnp.float32) + NEWTON_THIRD * square).astype(jnp.bfloat16)
        if step == ITERS - 1:
            mine = mm(pick, x_ref[chunk], NT)
            out_ref[1] = NEWTON_FIRST * mine + mm(mine.astype(jnp.bfloat16), poly, NT)
            break
        for q in range(0, chunks, 2):
            part = jnp.concatenate([source[q], source[q + 1]], axis=1)
            part = NEWTON_FIRST * part.astype(jnp.float32) + mm(poly, part, NN)
            if step == 0:
                part = part * scale
            part = part.astype(jnp.bfloat16)
            x_ref[q] = part[:, :LANES]
            x_ref[q + 1] = part[:, LANES:]
        source = x_ref


def newton(gathered, cols):
    return pl.pallas_call(
        newton_kernel,
        in_specs=[VMEM],
        out_specs=VMEM,
        out_shape=jax.ShapeDtypeStruct((2, cols, gathered.shape[1]), jnp.float32),
        scratch_shapes=[pltpu.VMEM(gathered.shape, jnp.bfloat16)],
        compiler_params=PARAMS,
    )(gathered)


def finish_kernel(factor, back_ref, weights_ref, new_ref, update_ref):
    mats, slab, _ = weights_ref.shape
    mine = pl.ds(pl.multiple_of(lax.axis_index("core") * slab, slab), slab)
    for m in range(mats):
        new_ref[m] = back_ref[m, 0, mine, :]
        update_ref[m] = factor * back_ref[m, 1, mine, :] + WEIGHT_DECAY * weights_ref[m]


def finish(back, weights, factor):
    def kernel(*refs):
        finish_kernel(factor, *refs)

    shape = jax.ShapeDtypeStruct(weights.shape, jnp.float32)
    return pl.pallas_call(
        kernel,
        in_specs=[VMEM, VMEM],
        out_specs=[VMEM, VMEM],
        out_shape=[shape, shape],
        compiler_params=PARAMS,
    )(back, weights)


def per_device(grads, momentum, weights, live_rows):
    mats, height, slab = momentum.shape
    cores = lax.axis_size("core")
    width = grads.shape[3]
    core = lax.axis_index("core")
    group = ("x", "y_low")
    given = lax.dynamic_index_in_dim(grads[0], cores - 1 - core, 0, keepdims=False)
    other = lax.ppermute(given, "core", [(0, 1), (1, 0)])
    old = lax.all_gather(jnp.swapaxes(momentum, 1, 2), "core")
    chunks = pair_sum(grads[0], other, old)
    chunks = lax.all_to_all(chunks, group, 0, 0)
    chunk = sum_and_copy(chunks, lax.axis_size("y_high"))
    chunk = lax.all_to_all(chunk, "y_high", 0, 0)
    copies = sum_mask_and_copy(mats, live_rows, chunk, width // LANES)
    gathered = lax.all_to_all(copies, group, 0, 0)
    mine = newton(gathered, cores * slab)
    back = lax.all_gather(mine, "core")
    new_momentum, update = finish(
        back, jnp.swapaxes(weights, 1, 2), UPDATE_SCALE * math.sqrt(width)
    )
    return (jnp.swapaxes(new_momentum, 1, 2), jnp.swapaxes(update, 1, 2))


def solution(mesh):
    fsdp, own = mesh.devices.shape
    assert (fsdp, own) == (64, 12)
    split = Mesh(mesh.devices.reshape(4, 4, 2, 2, own), ("x", "y_high", "y_low", "core", "own"))
    all_fsdp = ("x", "y_high", "y_low", "core")
    in_specs = (P(all_fsdp, "own", None, None), P("own", None, all_fsdp), P("own", None, all_fsdp), P())
    out_specs = (P("own", None, all_fsdp), P("own", None, all_fsdp))
    return jax.shard_map(
        per_device, mesh=split, in_specs=in_specs, out_specs=out_specs, check_vma=False
    )
```

```python
import functools
import math

import jax
import jax.numpy as jnp
from jax import lax
from jax.experimental import pallas as pl
from jax.experimental.pallas import tpu as pltpu
from jax.sharding import Mesh, PartitionSpec as P

ITERS = 5
MOMENTUM_DECAY = 0.95
NORM_EPS = 1e-07
NEWTON_FIRST = 3.4445
NEWTON_SECOND = -4.775
NEWTON_THIRD = 2.0315
UPDATE_SCALE = 0.2
WEIGHT_DECAY = 0.1

LANES = 128
VMEM = pl.BlockSpec(memory_space=pltpu.VMEM)
PARAMS = pltpu.CompilerParams(vmem_limit_bytes=32 * 1024 * 1024)
NT = (((1,), (1,)), ((), ()))
NN = (((1,), (0,)), ((), ()))
TN = (((0,), (0,)), ((), ()))

def chip_index():
    y = lax.axis_index("y_high") * lax.axis_size("y_low") + lax.axis_index("y_low")
    return lax.axis_index("x") * (lax.axis_size("y_high") * lax.axis_size("y_low")) + y


def mm(a, b, dims, precision=None):
    return lax.dot_general(a, b, dims, precision=precision, preferred_element_type=jnp.float32)


def pair_sum_kernel(own_ref, other_ref, old_ref, out_ref):
    core, chip = lax.axis_index("core"), chip_index()
    rows = out_ref.shape[1]
    for q in range(out_ref.shape[0]):
        lanes = slice(q * LANES, (q + 1) * LANES)
        total = own_ref[core, :rows, lanes].astype(jnp.float32) + other_ref[:rows, lanes].astype(jnp.float32)
        out_ref[q] = total.astype(jnp.bfloat16)
    cores, _, slab, height = old_ref.shape
    cols = cores * slab
    per_chunk = LANES // cols
    chunk, slot = chip // per_chunk, chip % per_chunk
    old = jnp.concatenate([old_ref[k, core] for k in range(cores)], axis=0)
    want = lax.broadcasted_iota(jnp.int32, (cols, LANES), 0) + slot * cols
    have = lax.broadcasted_iota(jnp.int32, (cols, LANES), 1)
    pick = (want == have).astype(jnp.float32)
    spread = mm(MOMENTUM_DECAY * old, pick, TN, lax.Precision.HIGHEST)[:rows]
    lanes = pl.ds(pl.multiple_of(chunk * LANES, LANES), LANES)
    total = own_ref[core, :rows, lanes].astype(jnp.float32) + other_ref[:rows, lanes].astype(jnp.float32)
    out_ref[chunk] = (total + spread).astype(jnp.bfloat16)


def pair_sum(own, other, old, rows):
    width = other.shape[1]
    return pl.pallas_call(
        pair_sum_kernel,
        in_specs=[VMEM, VMEM, VMEM],
        out_specs=VMEM,
        out_shape=jax.ShapeDtypeStruct((width // LANES, rows, LANES), jnp.bfloat16),
        compiler_params=PARAMS,
    )(own, other, old)


def add_parts(parts_ref):
    total = parts_ref[0].astype(jnp.float32)
    for k in range(1, parts_ref.shape[0]):
        total = total + parts_ref[k].astype(jnp.float32)
    return total


def sum_kernel(parts_ref, copies_ref):
    total = add_parts(parts_ref).astype(jnp.bfloat16)
    for k in range(copies_ref.shape[0]):
        copies_ref[k] = total


def sum_and_copy(parts, copies):
    return pl.pallas_call(
        sum_kernel,
        in_specs=[VMEM],
        out_specs=VMEM,
        out_shape=jax.ShapeDtypeStruct((copies,) + parts.shape[1:], jnp.bfloat16),
        compiler_params=PARAMS,
    )(parts)


def mask_kernel(mats, live_ref, parts_ref, copies_ref):
    total = add_parts(parts_ref)
    rows = lax.broadcasted_iota(jnp.int32, total.shape, 0)
    matrix = lax.axis_index("own") * mats + lax.axis_index("core")
    which = lax.broadcasted_iota(jnp.int32, live_ref.shape, 1) == matrix
    live = jnp.sum(jnp.where(which, live_ref[...], 0), axis=1, keepdims=True)
    new = jnp.where(rows < live, total, 0.0).astype(jnp.bfloat16)
    for k in range(copies_ref.shape[0]):
        copies_ref[k] = new


def sum_mask_and_copy(mats, live_rows, parts, copies):
    return pl.pallas_call(
        functools.partial(mask_kernel, mats),
        in_specs=[VMEM, VMEM],
        out_specs=VMEM,
        out_shape=jax.ShapeDtypeStruct((copies,) + parts.shape[1:], jnp.bfloat16),
        compiler_params=PARAMS,
    )(live_rows[None, :], parts)


def newton_kernel(gathered_ref, out_ref, x_ref):
    chunks, height, _ = gathered_ref.shape
    cols = out_ref.shape[1]
    per_chunk = LANES // cols
    chunk, slot = chip_index() // per_chunk, chip_index() % per_chunk
    want = lax.broadcasted_iota(jnp.int32, (cols, LANES), 0) + slot * cols
    have = lax.broadcasted_iota(jnp.int32, (cols, LANES), 1)
    pick = (want == have).astype(jnp.bfloat16)
    past = jnp.zeros((cols, out_ref.shape[2] - height), jnp.float32)

    def write(k, value):
        out_ref[k] = jnp.concatenate([value, past], axis=1) if past.shape[1] else value

    write(0, mm(pick, gathered_ref[chunk], NT))
    row = lax.broadcasted_iota(jnp.int32, (height, height), 0)
    col = lax.broadcasted_iota(jnp.int32, (height, height), 1)
    source = gathered_ref
    for step in range(ITERS):
        x = jnp.concatenate([source[q] for q in range(chunks)], axis=1)
        gram = mm(x, x, NT)
        if step == 0:
            norm = jnp.sqrt(jnp.sum(jnp.where(row == col, gram, 0.0), keepdims=True))
            scale = 1.0 / (norm + NORM_EPS)
            gram = gram * scale * scale
        gram = gram.astype(jnp.bfloat16)
        square = mm(gram, gram, NN)
        poly = (NEWTON_SECOND * gram.astype(jnp.float32) + NEWTON_THIRD * square).astype(jnp.bfloat16)
        if step == ITERS - 1:
            mine = mm(pick, x_ref[chunk], NT)
            write(1, NEWTON_FIRST * mine + mm(mine.astype(jnp.bfloat16), poly, NT))
            break
        for q in range(0, chunks, 2):
            part = jnp.concatenate([source[q], source[q + 1]], axis=1)
            part = NEWTON_FIRST * part.astype(jnp.float32) + mm(poly, part, NN)
            if step == 0:
                part = part * scale
            part = part.astype(jnp.bfloat16)
            x_ref[q] = part[:, :LANES]
            x_ref[q + 1] = part[:, LANES:]
        source = x_ref


def newton(gathered, cols, height):
    return pl.pallas_call(
        newton_kernel,
        in_specs=[VMEM],
        out_specs=VMEM,
        out_shape=jax.ShapeDtypeStruct((2, cols, height), jnp.float32),
        scratch_shapes=[pltpu.VMEM(gathered.shape, jnp.bfloat16)],
        compiler_params=PARAMS,
    )(gathered)


def finish_kernel(factor, back_ref, weights_ref, new_ref, update_ref):
    mats, slab, _ = weights_ref.shape
    mine = pl.ds(pl.multiple_of(lax.axis_index("core") * slab, slab), slab)
    for m in range(mats):
        new_ref[m] = back_ref[m, 0, mine, :]
        update_ref[m] = factor * back_ref[m, 1, mine, :] + WEIGHT_DECAY * weights_ref[m]


def finish(back, weights, factor):
    def kernel(*refs):
        finish_kernel(factor, *refs)

    shape = jax.ShapeDtypeStruct(weights.shape, jnp.float32)
    return pl.pallas_call(
        kernel,
        in_specs=[VMEM, VMEM],
        out_specs=[VMEM, VMEM],
        out_shape=[shape, shape],
        compiler_params=PARAMS,
    )(back, weights)


def per_device(grads, momentum, weights, live_rows):
    mats, height, slab = momentum.shape
    cores = lax.axis_size("core")
    width = grads.shape[3]
    core = lax.axis_index("core")
    group = ("x", "y_low")
    given = lax.dynamic_index_in_dim(grads[0], cores - 1 - core, 0, keepdims=False)
    other = lax.ppermute(given, "core", [(0, 1), (1, 0)])
    old = lax.all_gather(jnp.swapaxes(momentum, 1, 2), "core")
    def chain(rows):
        chunks = pair_sum(grads[0], other, old, rows)
        chunks = lax.all_to_all(chunks, group, 0, 0)
        chunk = sum_and_copy(chunks, lax.axis_size("y_high"))
        chunk = lax.all_to_all(chunk, "y_high", 0, 0)
        copies = sum_mask_and_copy(mats, live_rows, chunk, width // LANES)
        gathered = lax.all_to_all(copies, group, 0, 0)
        return newton(gathered, cores * slab, height)

    live = lax.dynamic_index_in_dim(live_rows, lax.axis_index("own") * mats + core, 0, keepdims=False)
    counts = [192, 240, height]
    level = sum((live > rows).astype(jnp.int32) for rows in counts[:-1])
    mine = lax.switch(level, [functools.partial(chain, rows) for rows in counts])
    back = lax.all_gather(mine, "core")
    new_momentum, update = finish(
        back, jnp.swapaxes(weights, 1, 2), UPDATE_SCALE * math.sqrt(width)
    )
    return (jnp.swapaxes(new_momentum, 1, 2), jnp.swapaxes(update, 1, 2))


def solution(mesh):
    fsdp, own = mesh.devices.shape
    assert (fsdp, own) == (64, 12)
    split = Mesh(mesh.devices.reshape(4, 4, 2, 2, own), ("x", "y_high", "y_low", "core", "own"))
    all_fsdp = ("x", "y_high", "y_low", "core")
    in_specs = (P(all_fsdp, "own", None, None), P("own", None, all_fsdp), P("own", None, all_fsdp), P())
    out_specs = (P("own", None, all_fsdp), P("own", None, all_fsdp))
    return jax.shard_map(
        per_device, mesh=split, in_specs=in_specs, out_specs=out_specs, check_vma=False
    )
```

```python
import functools
import math

import jax
import jax.numpy as jnp
from jax import lax
from jax.experimental import pallas as pl
from jax.experimental.pallas import tpu as pltpu
from jax.sharding import Mesh, PartitionSpec as P

ITERS = 5
MOMENTUM_DECAY = 0.95
NORM_EPS = 1e-07
NEWTON_FIRST = 3.4445
NEWTON_SECOND = -4.775
NEWTON_THIRD = 2.0315
UPDATE_SCALE = 0.2
WEIGHT_DECAY = 0.1

LANES = 128
VMEM = pl.BlockSpec(memory_space=pltpu.VMEM)
PARAMS = pltpu.CompilerParams(vmem_limit_bytes=32 * 1024 * 1024)
NT = (((1,), (1,)), ((), ()))
NN = (((1,), (0,)), ((), ()))
TN = (((0,), (0,)), ((), ()))

def chip_index():
    y = lax.axis_index("y_high") * lax.axis_size("y_low") + lax.axis_index("y_low")
    return lax.axis_index("x") * (lax.axis_size("y_high") * lax.axis_size("y_low")) + y


def mm(a, b, dims, precision=None):
    return lax.dot_general(a, b, dims, precision=precision, preferred_element_type=jnp.float32)


def spread_old(old):
    slab, _ = old.shape
    column = chip_index() * lax.axis_size("core") + lax.axis_index("core")
    per_chunk = LANES // slab
    want = lax.broadcasted_iota(jnp.int32, (slab, LANES), 0) + column % per_chunk * slab
    have = lax.broadcasted_iota(jnp.int32, (slab, LANES), 1)
    pick = (want == have).astype(jnp.float32)
    chunk = column // per_chunk
    lanes = pl.ds(pl.multiple_of(chunk * LANES, LANES), LANES)
    return mm(MOMENTUM_DECAY * old, pick, TN, lax.Precision.HIGHEST), chunk, lanes


def take_kernel(grads_ref, old_ref, out_ref):
    other = 1 - lax.axis_index("core")
    out_ref[...] = grads_ref[other]
    spread, _, lanes = spread_old(old_ref[other])
    out_ref[:, lanes] = (grads_ref[other, :, lanes].astype(jnp.float32) + spread).astype(jnp.bfloat16)


def take_other(grads, old):
    return pl.pallas_call(
        take_kernel,
        in_specs=[VMEM, VMEM],
        out_specs=VMEM,
        out_shape=jax.ShapeDtypeStruct(grads.shape[1:], grads.dtype),
        compiler_params=PARAMS,
    )(grads, old)


def pair_sum_kernel(own_ref, other_ref, old_ref, out_ref):
    core = lax.axis_index("core")
    rows = out_ref.shape[1]

    def total(lanes):
        return own_ref[core, :rows, lanes].astype(jnp.float32) + other_ref[:rows, lanes].astype(jnp.float32)

    for q in range(out_ref.shape[0]):
        out_ref[q] = total(slice(q * LANES, (q + 1) * LANES)).astype(jnp.bfloat16)
    spread, chunk, lanes = spread_old(old_ref[core])
    out_ref[chunk] = (total(lanes) + spread[:rows]).astype(jnp.bfloat16)


def pair_sum(own, other, old, rows):
    width = other.shape[1]
    return pl.pallas_call(
        pair_sum_kernel,
        in_specs=[VMEM, VMEM, VMEM],
        out_specs=VMEM,
        out_shape=jax.ShapeDtypeStruct((width // LANES, rows, LANES), jnp.bfloat16),
        compiler_params=PARAMS,
    )(own, other, old)


def add_parts(parts_ref):
    total = parts_ref[0].astype(jnp.float32)
    for k in range(1, parts_ref.shape[0]):
        total = total + parts_ref[k].astype(jnp.float32)
    return total


def sum_kernel(parts_ref, copies_ref):
    total = add_parts(parts_ref).astype(jnp.bfloat16)
    for k in range(copies_ref.shape[0]):
        copies_ref[k] = total


def sum_and_copy(parts, copies):
    return pl.pallas_call(
        sum_kernel,
        in_specs=[VMEM],
        out_specs=VMEM,
        out_shape=jax.ShapeDtypeStruct((copies,) + parts.shape[1:], jnp.bfloat16),
        compiler_params=PARAMS,
    )(parts)


def mask_kernel(mats, live_ref, parts_ref, copies_ref):
    total = add_parts(parts_ref)
    rows = lax.broadcasted_iota(jnp.int32, total.shape, 0)
    matrix = lax.axis_index("own") * mats + lax.axis_index("core")
    which = lax.broadcasted_iota(jnp.int32, live_ref.shape, 1) == matrix
    live = jnp.sum(jnp.where(which, live_ref[...], 0), axis=1, keepdims=True)
    new = jnp.where(rows < live, total, 0.0).astype(jnp.bfloat16)
    for k in range(copies_ref.shape[0]):
        copies_ref[k] = new


def sum_mask_and_copy(mats, live_rows, parts, copies):
    return pl.pallas_call(
        functools.partial(mask_kernel, mats),
        in_specs=[VMEM, VMEM],
        out_specs=VMEM,
        out_shape=jax.ShapeDtypeStruct((copies,) + parts.shape[1:], jnp.bfloat16),
        compiler_params=PARAMS,
    )(live_rows[None, :], parts)


def newton_kernel(gathered_ref, out_ref, x_ref):
    chunks, height, _ = gathered_ref.shape
    cols = out_ref.shape[1]
    per_chunk = LANES // cols
    chunk, slot = chip_index() // per_chunk, chip_index() % per_chunk
    want = lax.broadcasted_iota(jnp.int32, (cols, LANES), 0) + slot * cols
    have = lax.broadcasted_iota(jnp.int32, (cols, LANES), 1)
    pick = (want == have).astype(jnp.bfloat16)
    past = jnp.zeros((cols, out_ref.shape[2] - height), jnp.float32)

    def write(k, value):
        out_ref[k] = jnp.concatenate([value, past], axis=1) if past.shape[1] else value

    write(0, mm(pick, gathered_ref[chunk], NT))
    row = lax.broadcasted_iota(jnp.int32, (height, height), 0)
    col = lax.broadcasted_iota(jnp.int32, (height, height), 1)
    source = gathered_ref
    for step in range(ITERS):
        x = jnp.concatenate([source[q] for q in range(chunks)], axis=1)
        gram = mm(x, x, NT)
        if step == 0:
            norm = jnp.sqrt(jnp.sum(jnp.where(row == col, gram, 0.0), keepdims=True))
            scale = 1.0 / (norm + NORM_EPS)
            gram = gram * scale * scale
        gram = gram.astype(jnp.bfloat16)
        square = mm(gram, gram, NN)
        poly = (NEWTON_SECOND * gram.astype(jnp.float32) + NEWTON_THIRD * square).astype(jnp.bfloat16)
        if step == ITERS - 1:
            mine = mm(pick, x_ref[chunk], NT)
            write(1, NEWTON_FIRST * mine + mm(mine.astype(jnp.bfloat16), poly, NT))
            break
        for q in range(0, chunks, 2):
            part = jnp.concatenate([source[q], source[q + 1]], axis=1)
            part = NEWTON_FIRST * part.astype(jnp.float32) + mm(poly, part, NN)
            if step == 0:
                part = part * scale
            part = part.astype(jnp.bfloat16)
            x_ref[q] = part[:, :LANES]
            x_ref[q + 1] = part[:, LANES:]
        source = x_ref


def newton(gathered, cols, height):
    return pl.pallas_call(
        newton_kernel,
        in_specs=[VMEM],
        out_specs=VMEM,
        out_shape=jax.ShapeDtypeStruct((2, cols, height), jnp.float32),
        scratch_shapes=[pltpu.VMEM(gathered.shape, jnp.bfloat16)],
        compiler_params=PARAMS,
    )(gathered)


def finish_kernel(factor, back_ref, weights_ref, new_ref, update_ref):
    mats, slab, _ = weights_ref.shape
    mine = pl.ds(pl.multiple_of(lax.axis_index("core") * slab, slab), slab)
    for m in range(mats):
        new_ref[m] = back_ref[m, 0, mine, :]
        update_ref[m] = factor * back_ref[m, 1, mine, :] + WEIGHT_DECAY * weights_ref[m]


def finish(back, weights, factor):
    def kernel(*refs):
        finish_kernel(factor, *refs)

    shape = jax.ShapeDtypeStruct(weights.shape, jnp.float32)
    return pl.pallas_call(
        kernel,
        in_specs=[VMEM, VMEM],
        out_specs=[VMEM, VMEM],
        out_shape=[shape, shape],
        compiler_params=PARAMS,
    )(back, weights)


def per_device(grads, momentum, weights, live_rows):
    mats, height, slab = momentum.shape
    cores = lax.axis_size("core")
    width = grads.shape[3]
    core = lax.axis_index("core")
    group = ("x", "y_low")
    old = jnp.swapaxes(momentum, 1, 2)
    other = lax.ppermute(take_other(grads[0], old), "core", [(0, 1), (1, 0)])
    def chain(rows):
        chunks = pair_sum(grads[0], other, old, rows)
        chunks = lax.all_to_all(chunks, group, 0, 0)
        chunk = sum_and_copy(chunks, lax.axis_size("y_high"))
        chunk = lax.all_to_all(chunk, "y_high", 0, 0)
        copies = sum_mask_and_copy(mats, live_rows, chunk, width // LANES)
        gathered = lax.all_to_all(copies, group, 0, 0)
        return newton(gathered, cores * slab, height)

    live = lax.dynamic_index_in_dim(live_rows, lax.axis_index("own") * mats + core, 0, keepdims=False)
    counts = [192, 240, height]
    level = sum((live > rows).astype(jnp.int32) for rows in counts[:-1])
    mine = lax.switch(level, [functools.partial(chain, rows) for rows in counts])
    back = lax.all_gather(mine, "core")
    new_momentum, update = finish(
        back, jnp.swapaxes(weights, 1, 2), UPDATE_SCALE * math.sqrt(width)
    )
    return (jnp.swapaxes(new_momentum, 1, 2), jnp.swapaxes(update, 1, 2))


def solution(mesh):
    fsdp, own = mesh.devices.shape
    assert (fsdp, own) == (64, 12)
    split = Mesh(mesh.devices.reshape(4, 4, 2, 2, own), ("x", "y_high", "y_low", "core", "own"))
    all_fsdp = ("x", "y_high", "y_low", "core")
    in_specs = (P(all_fsdp, "own", None, None), P("own", None, all_fsdp), P("own", None, all_fsdp), P())
    out_specs = (P("own", None, all_fsdp), P("own", None, all_fsdp))
    return jax.shard_map(
        per_device, mesh=split, in_specs=in_specs, out_specs=out_specs, check_vma=False
    )
```

```python
import functools
import math

import jax
import jax.numpy as jnp
from jax import lax
from jax.experimental import pallas as pl
from jax.experimental.pallas import tpu as pltpu
from jax.sharding import Mesh, PartitionSpec as P

ITERS = 5
MOMENTUM_DECAY = 0.95
NORM_EPS = 1e-07
NEWTON_FIRST = 3.4445
NEWTON_SECOND = -4.775
NEWTON_THIRD = 2.0315
UPDATE_SCALE = 0.2
WEIGHT_DECAY = 0.1

LANES = 128
VMEM = pl.BlockSpec(memory_space=pltpu.VMEM)
PARAMS = pltpu.CompilerParams(vmem_limit_bytes=32 * 1024 * 1024)
NT = (((1,), (1,)), ((), ()))
NN = (((1,), (0,)), ((), ()))
TN = (((0,), (0,)), ((), ()))

def chip_index():
    y = lax.axis_index("y_high") * lax.axis_size("y_low") + lax.axis_index("y_low")
    return lax.axis_index("x") * (lax.axis_size("y_high") * lax.axis_size("y_low")) + y


def mm(a, b, dims, precision=None):
    return lax.dot_general(a, b, dims, precision=precision, preferred_element_type=jnp.float32)


def spread_old(old):
    slab, _ = old.shape
    column = chip_index() * lax.axis_size("core") + lax.axis_index("core")
    per_chunk = LANES // slab
    want = lax.broadcasted_iota(jnp.int32, (slab, LANES), 0) + column % per_chunk * slab
    have = lax.broadcasted_iota(jnp.int32, (slab, LANES), 1)
    pick = (want == have).astype(jnp.float32)
    chunk = column // per_chunk
    lanes = pl.ds(pl.multiple_of(chunk * LANES, LANES), LANES)
    return mm(MOMENTUM_DECAY * old, pick, TN, lax.Precision.HIGHEST), chunk, lanes


def take_kernel(grads_ref, old_ref, out_ref):
    other = 1 - lax.axis_index("core")
    out_ref[...] = grads_ref[other]
    spread, _, lanes = spread_old(old_ref[other])
    out_ref[:, lanes] = (grads_ref[other, :, lanes].astype(jnp.float32) + spread).astype(jnp.bfloat16)


def take_other(grads, old):
    return pl.pallas_call(
        take_kernel,
        in_specs=[VMEM, VMEM],
        out_specs=VMEM,
        out_shape=jax.ShapeDtypeStruct(grads.shape[1:], grads.dtype),
        compiler_params=PARAMS,
    )(grads, old)


def pair_sum_kernel(own_ref, other_ref, old_ref, out_ref):
    core = lax.axis_index("core")
    rows = out_ref.shape[1]

    def total(lanes):
        return own_ref[core, :rows, lanes].astype(jnp.float32) + other_ref[:rows, lanes].astype(jnp.float32)

    for q in range(out_ref.shape[0]):
        out_ref[q] = total(slice(q * LANES, (q + 1) * LANES)).astype(jnp.bfloat16)
    spread, chunk, lanes = spread_old(old_ref[core])
    out_ref[chunk] = (total(lanes) + spread[:rows]).astype(jnp.bfloat16)


def pair_sum(own, other, old, rows):
    width = other.shape[1]
    return pl.pallas_call(
        pair_sum_kernel,
        in_specs=[VMEM, VMEM, VMEM],
        out_specs=VMEM,
        out_shape=jax.ShapeDtypeStruct((width // LANES, rows, LANES), jnp.bfloat16),
        compiler_params=PARAMS,
    )(own, other, old)


def add_parts(parts_ref):
    total = parts_ref[0].astype(jnp.float32)
    for k in range(1, parts_ref.shape[0]):
        total = total + parts_ref[k].astype(jnp.float32)
    return total


def sum_kernel(parts_ref, copies_ref):
    total = add_parts(parts_ref).astype(jnp.bfloat16)
    for k in range(copies_ref.shape[0]):
        copies_ref[k] = total


def sum_and_copy(parts, copies):
    return pl.pallas_call(
        sum_kernel,
        in_specs=[VMEM],
        out_specs=VMEM,
        out_shape=jax.ShapeDtypeStruct((copies,) + parts.shape[1:], jnp.bfloat16),
        compiler_params=PARAMS,
    )(parts)


def mask_kernel(mats, live_ref, parts_ref, copies_ref):
    total = add_parts(parts_ref)
    rows = lax.broadcasted_iota(jnp.int32, total.shape, 0)
    matrix = lax.axis_index("own") * mats + lax.axis_index("core")
    which = lax.broadcasted_iota(jnp.int32, live_ref.shape, 1) == matrix
    live = jnp.sum(jnp.where(which, live_ref[...], 0), axis=1, keepdims=True)
    new = jnp.where(rows < live, total, 0.0).astype(jnp.bfloat16)
    for k in range(copies_ref.shape[0]):
        copies_ref[k] = new


def sum_mask_and_copy(mats, live_rows, parts, copies):
    return pl.pallas_call(
        functools.partial(mask_kernel, mats),
        in_specs=[VMEM, VMEM],
        out_specs=VMEM,
        out_shape=jax.ShapeDtypeStruct((copies,) + parts.shape[1:], jnp.bfloat16),
        compiler_params=PARAMS,
    )(live_rows[None, :], parts)


def newton_kernel(gathered_ref, out_ref, x_ref):
    chunks, height, _ = gathered_ref.shape
    cols = out_ref.shape[1]
    per_chunk = LANES // cols
    chunk, slot = chip_index() // per_chunk, chip_index() % per_chunk
    want = lax.broadcasted_iota(jnp.int32, (cols, LANES), 0) + slot * cols
    have = lax.broadcasted_iota(jnp.int32, (cols, LANES), 1)
    pick = (want == have).astype(jnp.bfloat16)
    past = jnp.zeros((cols, out_ref.shape[2] - height), jnp.float32)

    def write(k, value):
        out_ref[k] = jnp.concatenate([value, past], axis=1) if past.shape[1] else value

    write(0, mm(pick, gathered_ref[chunk], NT))
    row = lax.broadcasted_iota(jnp.int32, (height, height), 0)
    col = lax.broadcasted_iota(jnp.int32, (height, height), 1)
    source = gathered_ref
    for step in range(ITERS):
        x = jnp.concatenate([source[q] for q in range(chunks)], axis=1)
        gram = mm(x, x, NT)
        if step == 0:
            norm = jnp.sqrt(jnp.sum(jnp.where(row == col, gram, 0.0), keepdims=True))
            scale = 1.0 / (norm + NORM_EPS)
            gram = gram * scale * scale
        gram = gram.astype(jnp.bfloat16)
        square = mm(gram, gram, NN)
        poly = (NEWTON_SECOND * gram.astype(jnp.float32) + NEWTON_THIRD * square).astype(jnp.bfloat16)
        if step == ITERS - 1:
            mine = mm(pick, x_ref[chunk], NT)
            write(1, NEWTON_FIRST * mine + mm(mine.astype(jnp.bfloat16), poly, NT))
            break
        for q in range(0, chunks, 2):
            part = jnp.concatenate([source[q], source[q + 1]], axis=1)
            part = NEWTON_FIRST * part.astype(jnp.float32) + mm(poly, part, NN)
            if step == 0:
                part = part * scale
            part = part.astype(jnp.bfloat16)
            x_ref[q] = part[:, :LANES]
            x_ref[q + 1] = part[:, LANES:]
        source = x_ref


def newton(gathered, cols, height):
    return pl.pallas_call(
        newton_kernel,
        in_specs=[VMEM],
        out_specs=VMEM,
        out_shape=jax.ShapeDtypeStruct((2, cols, height), jnp.float32),
        scratch_shapes=[pltpu.VMEM(gathered.shape, jnp.bfloat16)],
        compiler_params=PARAMS,
    )(gathered)


def finish_kernel(factor, back_ref, weights_ref, new_ref, update_ref):
    mats, slab, _ = weights_ref.shape
    mine = pl.ds(pl.multiple_of(lax.axis_index("core") * slab, slab), slab)
    for m in range(mats):
        new_ref[m] = back_ref[m, 0, mine, :]
        update_ref[m] = factor * back_ref[m, 1, mine, :] + WEIGHT_DECAY * weights_ref[m]


def finish(back, weights, factor):
    def kernel(*refs):
        finish_kernel(factor, *refs)

    shape = jax.ShapeDtypeStruct(weights.shape, jnp.float32)
    return pl.pallas_call(
        kernel,
        in_specs=[VMEM, VMEM],
        out_specs=[VMEM, VMEM],
        out_shape=[shape, shape],
        compiler_params=PARAMS,
    )(back, weights)


def per_device(grads, momentum, weights, live_rows):
    mats, height, slab = momentum.shape
    cores = lax.axis_size("core")
    width = grads.shape[3]
    core = lax.axis_index("core")
    group = ("x", "y_low")
    old = jnp.swapaxes(momentum, 1, 2)
    other = lax.ppermute(take_other(grads[0], old), "core", [(0, 1), (1, 0)])
    def chain(rows):
        chunks = pair_sum(grads[0], other, old, rows)
        chunks = lax.all_to_all(chunks, group, 0, 0)
        chunk = sum_and_copy(chunks, lax.axis_size("y_high"))
        chunk = lax.all_to_all(chunk, "y_high", 0, 0)
        copies = sum_mask_and_copy(mats, live_rows, chunk, width // LANES)
        gathered = lax.all_to_all(copies, group, 0, 0)
        return newton(gathered, cores * slab, height)

    live = lax.dynamic_index_in_dim(live_rows, lax.axis_index("own") * mats + core, 0, keepdims=False)
    step, least = 16, 176
    counts = range(least, height + 1, step)
    level = jnp.maximum(live - least + step - 1, 0) // step
    mine = lax.switch(level, [functools.partial(chain, rows) for rows in counts])
    back = lax.all_gather(mine, "core")
    new_momentum, update = finish(
        back, jnp.swapaxes(weights, 1, 2), UPDATE_SCALE * math.sqrt(width)
    )
    return (jnp.swapaxes(new_momentum, 1, 2), jnp.swapaxes(update, 1, 2))


def solution(mesh):
    fsdp, own = mesh.devices.shape
    assert (fsdp, own) == (64, 12)
    split = Mesh(mesh.devices.reshape(4, 4, 2, 2, own), ("x", "y_high", "y_low", "core", "own"))
    all_fsdp = ("x", "y_high", "y_low", "core")
    in_specs = (P(all_fsdp, "own", None, None), P("own", None, all_fsdp), P("own", None, all_fsdp), P())
    out_specs = (P("own", None, all_fsdp), P("own", None, all_fsdp))
    return jax.shard_map(
        per_device, mesh=split, in_specs=in_specs, out_specs=out_specs, check_vma=False
    )
```

```python
import functools
import math

import jax
import jax.numpy as jnp
from jax import lax
from jax.experimental import pallas as pl
from jax.experimental.pallas import tpu as pltpu
from jax.sharding import Mesh, PartitionSpec as P

ITERS = 5
MOMENTUM_DECAY = 0.95
NORM_EPS = 1e-07
NEWTON_FIRST = 3.4445
NEWTON_SECOND = -4.775
NEWTON_THIRD = 2.0315
UPDATE_SCALE = 0.2
WEIGHT_DECAY = 0.1

LANES = 128
VMEM = pl.BlockSpec(memory_space=pltpu.VMEM)
PARAMS = pltpu.CompilerParams(vmem_limit_bytes=32 * 1024 * 1024)
NT = (((1,), (1,)), ((), ()))
NN = (((1,), (0,)), ((), ()))
TN = (((0,), (0,)), ((), ()))

def chip_index():
    y = lax.axis_index("y_high") * lax.axis_size("y_low") + lax.axis_index("y_low")
    return lax.axis_index("x") * (lax.axis_size("y_high") * lax.axis_size("y_low")) + y


def mm(a, b, dims, precision=None):
    return lax.dot_general(a, b, dims, precision=precision, preferred_element_type=jnp.float32)


def spread_old(old):
    slab, _ = old.shape
    column = chip_index() * lax.axis_size("core") + lax.axis_index("core")
    per_chunk = LANES // slab
    want = lax.broadcasted_iota(jnp.int32, (slab, LANES), 0) + column % per_chunk * slab
    have = lax.broadcasted_iota(jnp.int32, (slab, LANES), 1)
    pick = (want == have).astype(jnp.float32)
    chunk = column // per_chunk
    lanes = pl.ds(pl.multiple_of(chunk * LANES, LANES), LANES)
    return mm(MOMENTUM_DECAY * old, pick, TN, lax.Precision.HIGHEST), chunk, lanes


def take_kernel(grads_ref, old_ref, out_ref):
    other = 1 - lax.axis_index("core")
    out_ref[...] = grads_ref[other]
    spread, _, lanes = spread_old(old_ref[other])
    out_ref[:, lanes] = (grads_ref[other, :, lanes].astype(jnp.float32) + spread).astype(jnp.bfloat16)


def take_other(grads, old):
    return pl.pallas_call(
        take_kernel,
        in_specs=[VMEM, VMEM],
        out_specs=VMEM,
        out_shape=jax.ShapeDtypeStruct(grads.shape[1:], grads.dtype),
        compiler_params=PARAMS,
    )(grads, old)


def pair_sum_kernel(own_ref, other_ref, old_ref, out_ref):
    core = lax.axis_index("core")
    rows = out_ref.shape[1]

    def total(lanes):
        return own_ref[core, :rows, lanes].astype(jnp.float32) + other_ref[:rows, lanes].astype(jnp.float32)

    for q in range(out_ref.shape[0]):
        out_ref[q] = total(slice(q * LANES, (q + 1) * LANES)).astype(jnp.bfloat16)
    spread, chunk, lanes = spread_old(old_ref[core])
    out_ref[chunk] = (total(lanes) + spread[:rows]).astype(jnp.bfloat16)


def pair_sum(own, other, old, rows):
    width = other.shape[1]
    return pl.pallas_call(
        pair_sum_kernel,
        in_specs=[VMEM, VMEM, VMEM],
        out_specs=VMEM,
        out_shape=jax.ShapeDtypeStruct((width // LANES, rows, LANES), jnp.bfloat16),
        compiler_params=PARAMS,
    )(own, other, old)


def add_parts(parts_ref):
    total = parts_ref[0].astype(jnp.float32)
    for k in range(1, parts_ref.shape[0]):
        total = total + parts_ref[k].astype(jnp.float32)
    return total


def sum_kernel(parts_ref, copies_ref):
    total = add_parts(parts_ref).astype(jnp.bfloat16)
    for k in range(copies_ref.shape[0]):
        copies_ref[k] = total


def sum_and_copy(parts, copies):
    return pl.pallas_call(
        sum_kernel,
        in_specs=[VMEM],
        out_specs=VMEM,
        out_shape=jax.ShapeDtypeStruct((copies,) + parts.shape[1:], jnp.bfloat16),
        compiler_params=PARAMS,
    )(parts)


def mask_kernel(mats, live_ref, parts_ref, copies_ref):
    total = add_parts(parts_ref)
    rows = lax.broadcasted_iota(jnp.int32, total.shape, 0)
    matrix = lax.axis_index("own") * mats + lax.axis_index("core")
    which = lax.broadcasted_iota(jnp.int32, live_ref.shape, 1) == matrix
    live = jnp.sum(jnp.where(which, live_ref[...], 0), axis=1, keepdims=True)
    new = jnp.where(rows < live, total, 0.0).astype(jnp.bfloat16)
    for k in range(copies_ref.shape[0]):
        copies_ref[k] = new


def sum_mask_and_copy(mats, live_rows, parts, copies):
    return pl.pallas_call(
        functools.partial(mask_kernel, mats),
        in_specs=[VMEM, VMEM],
        out_specs=VMEM,
        out_shape=jax.ShapeDtypeStruct((copies,) + parts.shape[1:], jnp.bfloat16),
        compiler_params=PARAMS,
    )(live_rows[None, :], parts)


def newton_kernel(gathered_ref, out_ref, x_ref):
    chunks, height, _ = gathered_ref.shape
    cols = out_ref.shape[1]
    per_chunk = LANES // cols
    chunk, slot = chip_index() // per_chunk, chip_index() % per_chunk
    want = lax.broadcasted_iota(jnp.int32, (cols, LANES), 0) + slot * cols
    have = lax.broadcasted_iota(jnp.int32, (cols, LANES), 1)
    pick = (want == have).astype(jnp.bfloat16)
    past = jnp.zeros((cols, out_ref.shape[2] - height), jnp.float32)

    def write(k, value):
        out_ref[k] = jnp.concatenate([value, past], axis=1) if past.shape[1] else value

    write(0, mm(pick, gathered_ref[chunk], NT))
    row = lax.broadcasted_iota(jnp.int32, (height, height), 0)
    col = lax.broadcasted_iota(jnp.int32, (height, height), 1)
    source = gathered_ref
    for step in range(ITERS):
        x = jnp.concatenate([source[q] for q in range(chunks)], axis=1)
        gram = mm(x, x, NT)
        if step == 0:
            norm = jnp.sqrt(jnp.sum(jnp.where(row == col, gram, 0.0), keepdims=True))
            scale = 1.0 / (norm + NORM_EPS)
            gram = gram * scale * scale
        gram = gram.astype(jnp.bfloat16)
        square = mm(gram, gram, NN)
        poly = (NEWTON_SECOND * gram.astype(jnp.float32) + NEWTON_THIRD * square).astype(jnp.bfloat16)
        if step == ITERS - 1:
            mine = mm(pick, x_ref[chunk], NT)
            write(1, NEWTON_FIRST * mine + mm(mine.astype(jnp.bfloat16), poly, NT))
            break
        for q in range(0, chunks, 2):
            part = jnp.concatenate([source[q], source[q + 1]], axis=1)
            part = NEWTON_FIRST * part.astype(jnp.float32) + mm(poly, part, NN)
            if step == 0:
                part = part * scale
            part = part.astype(jnp.bfloat16)
            x_ref[q] = part[:, :LANES]
            x_ref[q + 1] = part[:, LANES:]
        source = x_ref


def newton(gathered, cols, height):
    return pl.pallas_call(
        newton_kernel,
        in_specs=[VMEM],
        out_specs=VMEM,
        out_shape=jax.ShapeDtypeStruct((2, cols, height), jnp.float32),
        scratch_shapes=[pltpu.VMEM(gathered.shape, jnp.bfloat16)],
        compiler_params=PARAMS,
    )(gathered)


def finish_kernel(factor, back_ref, weights_ref, new_ref, update_ref):
    mats, slab, _ = weights_ref.shape
    mine = pl.ds(pl.multiple_of(lax.axis_index("core") * slab, slab), slab)
    for m in range(mats):
        new_ref[m] = back_ref[m, 0, mine, :]
        update_ref[m] = factor * back_ref[m, 1, mine, :] + WEIGHT_DECAY * weights_ref[m]


def finish(back, weights, factor):
    def kernel(*refs):
        finish_kernel(factor, *refs)

    shape = jax.ShapeDtypeStruct(weights.shape, jnp.float32)
    return pl.pallas_call(
        kernel,
        in_specs=[VMEM, VMEM],
        out_specs=[VMEM, VMEM],
        out_shape=[shape, shape],
        compiler_params=PARAMS,
    )(back, weights)


def per_device(grads, momentum, weights, live_rows):
    mats, height, slab = momentum.shape
    cores = lax.axis_size("core")
    width = grads.shape[3]
    core = lax.axis_index("core")
    group = ("x", "y_low")
    old = jnp.swapaxes(momentum, 1, 2)
    other = lax.ppermute(take_other(grads[0], old), "core", [(0, 1), (1, 0)])
    def chain(rows):
        chunks = pair_sum(grads[0], other, old, rows)
        chunks = lax.all_to_all(chunks, group, 0, 0)
        chunk = sum_and_copy(chunks, lax.axis_size("y_high"))
        chunk = lax.all_to_all(chunk, "y_high", 0, 0)
        copies = sum_mask_and_copy(mats, live_rows, chunk, width // LANES)
        gathered = lax.all_to_all(copies, group, 0, 0)
        return newton(gathered, cores * slab, height)

    live = lax.dynamic_index_in_dim(live_rows, lax.axis_index("own") * mats + core, 0, keepdims=False)
    step, least = 32, 192
    counts = range(least, height + 1, step)
    level = jnp.maximum(live - least + step - 1, 0) // step
    mine = lax.switch(level, [functools.partial(chain, rows) for rows in counts])
    back = lax.all_gather(mine, "core")
    new_momentum, update = finish(
        back, jnp.swapaxes(weights, 1, 2), UPDATE_SCALE * math.sqrt(width)
    )
    return (jnp.swapaxes(new_momentum, 1, 2), jnp.swapaxes(update, 1, 2))


def solution(mesh):
    fsdp, own = mesh.devices.shape
    assert (fsdp, own) == (64, 12)
    split = Mesh(mesh.devices.reshape(4, 4, 2, 2, own), ("x", "y_high", "y_low", "core", "own"))
    all_fsdp = ("x", "y_high", "y_low", "core")
    in_specs = (P(all_fsdp, "own", None, None), P("own", None, all_fsdp), P("own", None, all_fsdp), P())
    out_specs = (P("own", None, all_fsdp), P("own", None, all_fsdp))
    return jax.shard_map(
        per_device, mesh=split, in_specs=in_specs, out_specs=out_specs, check_vma=False
    )
```

```python
import functools
import math

import jax
import jax.numpy as jnp
from jax import lax
from jax.experimental import pallas as pl
from jax.experimental.pallas import tpu as pltpu
from jax.sharding import Mesh, PartitionSpec as P

ITERS = 5
MOMENTUM_DECAY = 0.95
NORM_EPS = 1e-07
NEWTON_FIRST = 3.4445
NEWTON_SECOND = -4.775
NEWTON_THIRD = 2.0315
UPDATE_SCALE = 0.2
WEIGHT_DECAY = 0.1

LANES = 128
VMEM = pl.BlockSpec(memory_space=pltpu.VMEM)
PARAMS = pltpu.CompilerParams(vmem_limit_bytes=32 * 1024 * 1024)
NT = (((1,), (1,)), ((), ()))
NN = (((1,), (0,)), ((), ()))
TN = (((0,), (0,)), ((), ()))

def chip_index():
    y = lax.axis_index("y_high") * lax.axis_size("y_low") + lax.axis_index("y_low")
    return lax.axis_index("x") * (lax.axis_size("y_high") * lax.axis_size("y_low")) + y


def mm(a, b, dims, precision=None):
    return lax.dot_general(a, b, dims, precision=precision, preferred_element_type=jnp.float32)


def live_pair(live_ref):
    first = lax.axis_index("own") * 2
    ids = lax.broadcasted_iota(jnp.int32, live_ref.shape, 1)
    rows = [jnp.where(ids == first + m, live_ref[...], 0) for m in range(2)]
    return [jnp.sum(r, axis=1, keepdims=True) for r in rows]


def swapped(live_ref):
    low, high = live_pair(live_ref)
    return (low > high).astype(jnp.int32)[0, 0]


def spread_old(old):
    slab, _ = old.shape
    column = chip_index() * lax.axis_size("core") + lax.axis_index("core")
    per_chunk = LANES // slab
    want = lax.broadcasted_iota(jnp.int32, (slab, LANES), 0) + column % per_chunk * slab
    have = lax.broadcasted_iota(jnp.int32, (slab, LANES), 1)
    pick = (want == have).astype(jnp.float32)
    chunk = column // per_chunk
    lanes = pl.ds(pl.multiple_of(chunk * LANES, LANES), LANES)
    return mm(MOMENTUM_DECAY * old, pick, TN, lax.Precision.HIGHEST), chunk, lanes


def take_kernel(live_ref, grads_ref, old_ref, out_ref):
    other = (lax.axis_index("core") + 1 + swapped(live_ref)) % 2
    out_ref[...] = grads_ref[other]
    spread, _, lanes = spread_old(old_ref[other])
    out_ref[:, lanes] = (grads_ref[other, :, lanes].astype(jnp.float32) + spread).astype(jnp.bfloat16)


def take_other(live, grads, old):
    return pl.pallas_call(
        take_kernel,
        in_specs=[VMEM, VMEM, VMEM],
        out_specs=VMEM,
        out_shape=jax.ShapeDtypeStruct(grads.shape[1:], grads.dtype),
        compiler_params=PARAMS,
    )(live, grads, old)


def pair_sum_kernel(live_ref, own_ref, other_ref, old_ref, out_ref):
    held = (lax.axis_index("core") + swapped(live_ref)) % 2
    rows = out_ref.shape[1]

    def total(lanes):
        return own_ref[held, :rows, lanes].astype(jnp.float32) + other_ref[:rows, lanes].astype(jnp.float32)

    for q in range(out_ref.shape[0]):
        out_ref[q] = total(slice(q * LANES, (q + 1) * LANES)).astype(jnp.bfloat16)
    spread, chunk, lanes = spread_old(old_ref[held])
    out_ref[chunk] = (total(lanes) + spread[:rows]).astype(jnp.bfloat16)


def pair_sum(live, own, other, old, rows):
    width = other.shape[1]
    return pl.pallas_call(
        pair_sum_kernel,
        in_specs=[VMEM, VMEM, VMEM, VMEM],
        out_specs=VMEM,
        out_shape=jax.ShapeDtypeStruct((width // LANES, rows, LANES), jnp.bfloat16),
        compiler_params=PARAMS,
    )(live, own, other, old)


def add_parts(parts_ref):
    total = parts_ref[0].astype(jnp.float32)
    for k in range(1, parts_ref.shape[0]):
        total = total + parts_ref[k].astype(jnp.float32)
    return total


def sum_kernel(parts_ref, copies_ref):
    total = add_parts(parts_ref).astype(jnp.bfloat16)
    for k in range(copies_ref.shape[0]):
        copies_ref[k] = total


def sum_and_copy(parts, copies):
    return pl.pallas_call(
        sum_kernel,
        in_specs=[VMEM],
        out_specs=VMEM,
        out_shape=jax.ShapeDtypeStruct((copies,) + parts.shape[1:], jnp.bfloat16),
        compiler_params=PARAMS,
    )(parts)


def mask_kernel(live_ref, parts_ref, copies_ref):
    total = add_parts(parts_ref)
    rows = lax.broadcasted_iota(jnp.int32, total.shape, 0)
    low, high = live_pair(live_ref)
    live = jnp.where(lax.axis_index("core") == 0, jnp.minimum(low, high), jnp.maximum(low, high))
    new = jnp.where(rows < live, total, 0.0).astype(jnp.bfloat16)
    for k in range(copies_ref.shape[0]):
        copies_ref[k] = new


def sum_mask_and_copy(live, parts, copies):
    return pl.pallas_call(
        mask_kernel,
        in_specs=[VMEM, VMEM],
        out_specs=VMEM,
        out_shape=jax.ShapeDtypeStruct((copies,) + parts.shape[1:], jnp.bfloat16),
        compiler_params=PARAMS,
    )(live, parts)


def newton_kernel(gathered_ref, out_ref, x_ref):
    chunks, height, _ = gathered_ref.shape
    cols = out_ref.shape[1]
    per_chunk = LANES // cols
    chunk, slot = chip_index() // per_chunk, chip_index() % per_chunk
    want = lax.broadcasted_iota(jnp.int32, (cols, LANES), 0) + slot * cols
    have = lax.broadcasted_iota(jnp.int32, (cols, LANES), 1)
    pick = (want == have).astype(jnp.bfloat16)
    past = jnp.zeros((cols, out_ref.shape[2] - height), jnp.float32)

    def write(k, value):
        out_ref[k] = jnp.concatenate([value, past], axis=1) if past.shape[1] else value

    write(0, mm(pick, gathered_ref[chunk], NT))
    row = lax.broadcasted_iota(jnp.int32, (height, height), 0)
    col = lax.broadcasted_iota(jnp.int32, (height, height), 1)
    source = gathered_ref
    for step in range(ITERS):
        x = jnp.concatenate([source[q] for q in range(chunks)], axis=1)
        gram = mm(x, x, NT)
        if step == 0:
            norm = jnp.sqrt(jnp.sum(jnp.where(row == col, gram, 0.0), keepdims=True))
            scale = 1.0 / (norm + NORM_EPS)
            gram = gram * scale * scale
        gram = gram.astype(jnp.bfloat16)
        square = mm(gram, gram, NN)
        poly = (NEWTON_SECOND * gram.astype(jnp.float32) + NEWTON_THIRD * square).astype(jnp.bfloat16)
        if step == ITERS - 1:
            mine = mm(pick, x_ref[chunk], NT)
            write(1, NEWTON_FIRST * mine + mm(mine.astype(jnp.bfloat16), poly, NT))
            break
        for q in range(0, chunks, 2):
            part = jnp.concatenate([source[q], source[q + 1]], axis=1)
            part = NEWTON_FIRST * part.astype(jnp.float32) + mm(poly, part, NN)
            if step == 0:
                part = part * scale
            part = part.astype(jnp.bfloat16)
            x_ref[q] = part[:, :LANES]
            x_ref[q + 1] = part[:, LANES:]
        source = x_ref


def newton(gathered, cols, height):
    return pl.pallas_call(
        newton_kernel,
        in_specs=[VMEM],
        out_specs=VMEM,
        out_shape=jax.ShapeDtypeStruct((2, cols, height), jnp.float32),
        scratch_shapes=[pltpu.VMEM(gathered.shape, jnp.bfloat16)],
        compiler_params=PARAMS,
    )(gathered)


def finish_kernel(factor, live_ref, back_ref, weights_ref, new_ref, update_ref):
    swap = swapped(live_ref)
    mats, slab, _ = weights_ref.shape
    mine = pl.ds(pl.multiple_of(lax.axis_index("core") * slab, slab), slab)
    for m in range(mats):
        holder = (m + swap) % 2
        new_ref[m] = back_ref[holder, 0, mine, :]
        update_ref[m] = factor * back_ref[holder, 1, mine, :] + WEIGHT_DECAY * weights_ref[m]


def finish(live, back, weights, factor):
    def kernel(*refs):
        finish_kernel(factor, *refs)

    shape = jax.ShapeDtypeStruct(weights.shape, jnp.float32)
    return pl.pallas_call(
        kernel,
        in_specs=[VMEM, VMEM, VMEM],
        out_specs=[VMEM, VMEM],
        out_shape=[shape, shape],
        compiler_params=PARAMS,
    )(live, back, weights)


def per_device(grads, momentum, weights, live_rows):
    mats, height, slab = momentum.shape
    cores = lax.axis_size("core")
    width = grads.shape[3]
    core = lax.axis_index("core")
    group = ("x", "y_low")
    live = live_rows[None, :]
    old = jnp.swapaxes(momentum, 1, 2)
    other = lax.ppermute(take_other(live, grads[0], old), "core", [(0, 1), (1, 0)])
    def chain(rows):
        chunks = pair_sum(live, grads[0], other, old, rows)
        chunks = lax.all_to_all(chunks, group, 0, 0)
        chunk = sum_and_copy(chunks, lax.axis_size("y_high"))
        chunk = lax.all_to_all(chunk, "y_high", 0, 0)
        copies = sum_mask_and_copy(live, chunk, width // LANES)
        gathered = lax.all_to_all(copies, group, 0, 0)
        return newton(gathered, cores * slab, height)

    pair = lax.dynamic_slice_in_dim(live_rows, lax.axis_index("own") * mats, mats)
    held = jnp.where(core == 0, jnp.min(pair), jnp.max(pair))
    step, least = 32, 192
    counts = range(least, height + 1, step)
    level = jnp.maximum(held - least + step - 1, 0) // step
    mine = lax.switch(level, [functools.partial(chain, rows) for rows in counts])
    back = lax.all_gather(mine, "core")
    new_momentum, update = finish(
        live, back, jnp.swapaxes(weights, 1, 2), UPDATE_SCALE * math.sqrt(width)
    )
    return (jnp.swapaxes(new_momentum, 1, 2), jnp.swapaxes(update, 1, 2))


def solution(mesh):
    fsdp, own = mesh.devices.shape
    assert (fsdp, own) == (64, 12)
    split = Mesh(mesh.devices.reshape(4, 4, 2, 2, own), ("x", "y_high", "y_low", "core", "own"))
    all_fsdp = ("x", "y_high", "y_low", "core")
    in_specs = (P(all_fsdp, "own", None, None), P("own", None, all_fsdp), P("own", None, all_fsdp), P())
    out_specs = (P("own", None, all_fsdp), P("own", None, all_fsdp))
    return jax.shard_map(
        per_device, mesh=split, in_specs=in_specs, out_specs=out_specs, check_vma=False
    )
```

```python
import functools
import math

import jax
import jax.numpy as jnp
from jax import lax
from jax.experimental import pallas as pl
from jax.experimental.pallas import tpu as pltpu
from jax.sharding import Mesh, PartitionSpec as P

ITERS = 5
MOMENTUM_DECAY = 0.95
NORM_EPS = 1e-07
NEWTON_FIRST = 3.4445
NEWTON_SECOND = -4.775
NEWTON_THIRD = 2.0315
UPDATE_SCALE = 0.2
WEIGHT_DECAY = 0.1

LANES = 128
VMEM = pl.BlockSpec(memory_space=pltpu.VMEM)
PARAMS = pltpu.CompilerParams(vmem_limit_bytes=32 * 1024 * 1024)
NT = (((1,), (1,)), ((), ()))
NN = (((1,), (0,)), ((), ()))
TN = (((0,), (0,)), ((), ()))

def chip_index():
    y = lax.axis_index("y_high") * lax.axis_size("y_low") + lax.axis_index("y_low")
    return lax.axis_index("x") * (lax.axis_size("y_high") * lax.axis_size("y_low")) + y


def mm(a, b, dims, precision=None):
    return lax.dot_general(a, b, dims, precision=precision, preferred_element_type=jnp.float32)


def spread_old(old):
    slab, _ = old.shape
    column = chip_index() * lax.axis_size("core") + lax.axis_index("core")
    per_chunk = LANES // slab
    want = lax.broadcasted_iota(jnp.int32, (slab, LANES), 0) + column % per_chunk * slab
    have = lax.broadcasted_iota(jnp.int32, (slab, LANES), 1)
    pick = (want == have).astype(jnp.float32)
    chunk = column // per_chunk
    lanes = pl.ds(pl.multiple_of(chunk * LANES, LANES), LANES)
    return mm(MOMENTUM_DECAY * old, pick, TN, lax.Precision.HIGHEST), chunk, lanes


def take_kernel(grads_ref, old_ref, out_ref):
    other = 1 - lax.axis_index("core")
    out_ref[...] = grads_ref[other]
    spread, _, lanes = spread_old(old_ref[other])
    out_ref[:, lanes] = (grads_ref[other, :, lanes].astype(jnp.float32) + spread).astype(jnp.bfloat16)


def take_other(grads, old):
    return pl.pallas_call(
        take_kernel,
        in_specs=[VMEM, VMEM],
        out_specs=VMEM,
        out_shape=jax.ShapeDtypeStruct(grads.shape[1:], grads.dtype),
        compiler_params=PARAMS,
    )(grads, old)


def pair_sum_kernel(own_ref, other_ref, old_ref, out_ref):
    core = lax.axis_index("core")
    rows = out_ref.shape[1]

    def total(lanes):
        return own_ref[core, :rows, lanes].astype(jnp.float32) + other_ref[:rows, lanes].astype(jnp.float32)

    for q in range(out_ref.shape[0]):
        out_ref[q] = total(slice(q * LANES, (q + 1) * LANES)).astype(jnp.bfloat16)
    spread, chunk, lanes = spread_old(old_ref[core])
    out_ref[chunk] = (total(lanes) + spread[:rows]).astype(jnp.bfloat16)


def pair_sum(own, other, old, rows):
    width = other.shape[1]
    return pl.pallas_call(
        pair_sum_kernel,
        in_specs=[VMEM, VMEM, VMEM],
        out_specs=VMEM,
        out_shape=jax.ShapeDtypeStruct((width // LANES, rows, LANES), jnp.bfloat16),
        compiler_params=PARAMS,
    )(own, other, old)


def add_parts(parts_ref):
    total = parts_ref[0].astype(jnp.float32)
    for k in range(1, parts_ref.shape[0]):
        total = total + parts_ref[k].astype(jnp.float32)
    return total


def sum_kernel(parts_ref, copies_ref):
    total = add_parts(parts_ref).astype(jnp.bfloat16)
    for k in range(copies_ref.shape[0]):
        copies_ref[k] = total


def sum_and_copy(parts, copies):
    return pl.pallas_call(
        sum_kernel,
        in_specs=[VMEM],
        out_specs=VMEM,
        out_shape=jax.ShapeDtypeStruct((copies,) + parts.shape[1:], jnp.bfloat16),
        compiler_params=PARAMS,
    )(parts)


def mask_kernel(mats, live_ref, parts_ref, copies_ref):
    total = add_parts(parts_ref)
    rows = lax.broadcasted_iota(jnp.int32, total.shape, 0)
    matrix = lax.axis_index("own") * mats + lax.axis_index("core")
    which = lax.broadcasted_iota(jnp.int32, live_ref.shape, 1) == matrix
    live = jnp.sum(jnp.where(which, live_ref[...], 0), axis=1, keepdims=True)
    new = jnp.where(rows < live, total, 0.0).astype(jnp.bfloat16)
    for k in range(copies_ref.shape[0]):
        copies_ref[k] = new


def sum_mask_and_copy(mats, live_rows, parts, copies):
    return pl.pallas_call(
        functools.partial(mask_kernel, mats),
        in_specs=[VMEM, VMEM],
        out_specs=VMEM,
        out_shape=jax.ShapeDtypeStruct((copies,) + parts.shape[1:], jnp.bfloat16),
        compiler_params=PARAMS,
    )(live_rows[None, :], parts)


def newton_kernel(gathered_ref, out_ref, x_ref):
    chunks, height, _ = gathered_ref.shape
    cols = out_ref.shape[1]
    per_chunk = LANES // cols
    chunk, slot = chip_index() // per_chunk, chip_index() % per_chunk
    want = lax.broadcasted_iota(jnp.int32, (cols, LANES), 0) + slot * cols
    have = lax.broadcasted_iota(jnp.int32, (cols, LANES), 1)
    pick = (want == have).astype(jnp.bfloat16)
    past = jnp.zeros((cols, out_ref.shape[2] - height), jnp.float32)

    def write(k, value):
        out_ref[k] = jnp.concatenate([value, past], axis=1) if past.shape[1] else value

    write(0, mm(pick, gathered_ref[chunk], NT))
    row = lax.broadcasted_iota(jnp.int32, (height, height), 0)
    col = lax.broadcasted_iota(jnp.int32, (height, height), 1)
    source = gathered_ref
    for step in range(ITERS):
        x = jnp.concatenate([source[q] for q in range(chunks)], axis=1)
        gram = mm(x, x, NT)
        if step == 0:
            norm = jnp.sqrt(jnp.sum(jnp.where(row == col, gram, 0.0), keepdims=True))
            scale = 1.0 / (norm + NORM_EPS)
            gram = gram * scale * scale
        gram = gram.astype(jnp.bfloat16)
        square = mm(gram, gram, NN)
        poly = (NEWTON_SECOND * gram.astype(jnp.float32) + NEWTON_THIRD * square).astype(jnp.bfloat16)
        if step == ITERS - 1:
            mine = mm(pick, x_ref[chunk], NT)
            write(1, NEWTON_FIRST * mine + mm(mine.astype(jnp.bfloat16), poly, NT))
            break
        for q in range(0, chunks, 2):
            part = jnp.concatenate([source[q], source[q + 1]], axis=1)
            part = NEWTON_FIRST * part.astype(jnp.float32) + mm(poly, part, NN)
            if step == 0:
                part = part * scale
            part = part.astype(jnp.bfloat16)
            x_ref[q] = part[:, :LANES]
            x_ref[q + 1] = part[:, LANES:]
        source = x_ref


def newton(gathered, cols, height):
    return pl.pallas_call(
        newton_kernel,
        in_specs=[VMEM],
        out_specs=VMEM,
        out_shape=jax.ShapeDtypeStruct((2, cols, height), jnp.float32),
        scratch_shapes=[pltpu.VMEM(gathered.shape, jnp.bfloat16)],
        compiler_params=PARAMS,
    )(gathered)


def finish_kernel(factor, back_ref, weights_ref, new_ref, update_ref):
    mats, slab, _ = weights_ref.shape
    mine = pl.ds(pl.multiple_of(lax.axis_index("core") * slab, slab), slab)
    for m in range(mats):
        new_ref[m] = back_ref[m, 0, mine, :]
        update_ref[m] = factor * back_ref[m, 1, mine, :] + WEIGHT_DECAY * weights_ref[m]


def finish(back, weights, factor):
    def kernel(*refs):
        finish_kernel(factor, *refs)

    shape = jax.ShapeDtypeStruct(weights.shape, jnp.float32)
    return pl.pallas_call(
        kernel,
        in_specs=[VMEM, VMEM],
        out_specs=[VMEM, VMEM],
        out_shape=[shape, shape],
        compiler_params=PARAMS,
    )(back, weights)


def per_device(grads, momentum, weights, live_rows):
    mats, height, slab = momentum.shape
    cores = lax.axis_size("core")
    width = grads.shape[3]
    core = lax.axis_index("core")
    group = ("x", "y_low")
    old = jnp.swapaxes(momentum, 1, 2)
    other = lax.ppermute(take_other(grads[0], old), "core", [(0, 1), (1, 0)])
    def chain(rows):
        chunks = pair_sum(grads[0], other, old, rows)
        chunks = lax.all_to_all(chunks, group, 0, 0)
        chunk = sum_and_copy(chunks, lax.axis_size("y_high"))
        chunk = lax.all_to_all(chunk, "y_high", 0, 0)
        copies = sum_mask_and_copy(mats, live_rows, chunk, width // LANES)
        gathered = lax.all_to_all(copies, group, 0, 0)
        return newton(gathered, cores * slab, height)

    live = lax.dynamic_index_in_dim(live_rows, lax.axis_index("own") * mats + core, 0, keepdims=False)
    step, least = 16, 192
    counts = range(least, height + 1, step)
    level = jnp.maximum(live - least + step - 1, 0) // step
    mine = lax.switch(level, [functools.partial(chain, rows) for rows in counts])
    back = lax.all_gather(mine, "core")
    new_momentum, update = finish(
        back, jnp.swapaxes(weights, 1, 2), UPDATE_SCALE * math.sqrt(width)
    )
    return (jnp.swapaxes(new_momentum, 1, 2), jnp.swapaxes(update, 1, 2))


def solution(mesh):
    fsdp, own = mesh.devices.shape
    assert (fsdp, own) == (64, 12)
    split = Mesh(mesh.devices.reshape(4, 4, 2, 2, own), ("x", "y_high", "y_low", "core", "own"))
    all_fsdp = ("x", "y_high", "y_low", "core")
    in_specs = (P(all_fsdp, "own", None, None), P("own", None, all_fsdp), P("own", None, all_fsdp), P())
    out_specs = (P("own", None, all_fsdp), P("own", None, all_fsdp))
    return jax.shard_map(
        per_device, mesh=split, in_specs=in_specs, out_specs=out_specs, check_vma=False
    )
```

```python
import functools
import math

import jax
import jax.numpy as jnp
from jax import lax
from jax.experimental import pallas as pl
from jax.experimental.pallas import tpu as pltpu
from jax.sharding import Mesh, PartitionSpec as P

ITERS = 5
MOMENTUM_DECAY = 0.95
NORM_EPS = 1e-07
NEWTON_FIRST = 3.4445
NEWTON_SECOND = -4.775
NEWTON_THIRD = 2.0315
UPDATE_SCALE = 0.2
WEIGHT_DECAY = 0.1

LANES = 128
VMEM = pl.BlockSpec(memory_space=pltpu.VMEM)
PARAMS = pltpu.CompilerParams(vmem_limit_bytes=32 * 1024 * 1024)
NT = (((1,), (1,)), ((), ()))
NN = (((1,), (0,)), ((), ()))
TN = (((0,), (0,)), ((), ()))

def chip_index():
    y = lax.axis_index("y_high") * lax.axis_size("y_low") + lax.axis_index("y_low")
    return lax.axis_index("x") * (lax.axis_size("y_high") * lax.axis_size("y_low")) + y


def mm(a, b, dims, precision=None):
    return lax.dot_general(a, b, dims, precision=precision, preferred_element_type=jnp.float32)


def spread_old(old):
    slab, _ = old.shape
    column = chip_index() * lax.axis_size("core") + lax.axis_index("core")
    per_chunk = LANES // slab
    want = lax.broadcasted_iota(jnp.int32, (slab, LANES), 0) + column % per_chunk * slab
    have = lax.broadcasted_iota(jnp.int32, (slab, LANES), 1)
    pick = (want == have).astype(jnp.float32)
    chunk = column // per_chunk
    lanes = pl.ds(pl.multiple_of(chunk * LANES, LANES), LANES)
    return mm(MOMENTUM_DECAY * old, pick, TN, lax.Precision.HIGHEST), chunk, lanes


def take_kernel(grads_ref, old_ref, out_ref):
    other = 1 - lax.axis_index("core")
    out_ref[...] = grads_ref[other]
    spread, _, lanes = spread_old(old_ref[other])
    out_ref[:, lanes] = (grads_ref[other, :, lanes].astype(jnp.float32) + spread).astype(jnp.bfloat16)


def take_other(grads, old):
    return pl.pallas_call(
        take_kernel,
        in_specs=[VMEM, VMEM],
        out_specs=VMEM,
        out_shape=jax.ShapeDtypeStruct(grads.shape[1:], grads.dtype),
        compiler_params=PARAMS,
    )(grads, old)


def pair_sum_kernel(own_ref, other_ref, old_ref, out_ref):
    core = lax.axis_index("core")
    rows = out_ref.shape[1]

    def total(lanes):
        return own_ref[core, :rows, lanes].astype(jnp.float32) + other_ref[:rows, lanes].astype(jnp.float32)

    for q in range(out_ref.shape[0]):
        out_ref[q] = total(slice(q * LANES, (q + 1) * LANES)).astype(jnp.bfloat16)
    spread, chunk, lanes = spread_old(old_ref[core])
    out_ref[chunk] = (total(lanes) + spread[:rows]).astype(jnp.bfloat16)


def pair_sum(own, other, old, rows):
    width = other.shape[1]
    return pl.pallas_call(
        pair_sum_kernel,
        in_specs=[VMEM, VMEM, VMEM],
        out_specs=VMEM,
        out_shape=jax.ShapeDtypeStruct((width // LANES, rows, LANES), jnp.bfloat16),
        compiler_params=PARAMS,
    )(own, other, old)


def add_parts(parts_ref):
    total = parts_ref[0].astype(jnp.float32)
    for k in range(1, parts_ref.shape[0]):
        total = total + parts_ref[k].astype(jnp.float32)
    return total


def sum_kernel(parts_ref, copies_ref):
    total = add_parts(parts_ref).astype(jnp.bfloat16)
    for k in range(copies_ref.shape[0]):
        copies_ref[k] = total


def sum_and_copy(parts, copies):
    return pl.pallas_call(
        sum_kernel,
        in_specs=[VMEM],
        out_specs=VMEM,
        out_shape=jax.ShapeDtypeStruct((copies,) + parts.shape[1:], jnp.bfloat16),
        compiler_params=PARAMS,
    )(parts)


def mask_kernel(mats, live_ref, parts_ref, copies_ref):
    total = add_parts(parts_ref)
    rows = lax.broadcasted_iota(jnp.int32, total.shape, 0)
    matrix = lax.axis_index("own") * mats + lax.axis_index("core")
    which = lax.broadcasted_iota(jnp.int32, live_ref.shape, 1) == matrix
    live = jnp.sum(jnp.where(which, live_ref[...], 0), axis=1, keepdims=True)
    new = jnp.where(rows < live, total, 0.0).astype(jnp.bfloat16)
    for k in range(copies_ref.shape[0]):
        copies_ref[k] = new


def sum_mask_and_copy(mats, live_rows, parts, copies):
    return pl.pallas_call(
        functools.partial(mask_kernel, mats),
        in_specs=[VMEM, VMEM],
        out_specs=VMEM,
        out_shape=jax.ShapeDtypeStruct((copies,) + parts.shape[1:], jnp.bfloat16),
        compiler_params=PARAMS,
    )(live_rows[None, :], parts)


def newton_kernel(gathered_ref, out_ref, x_ref):
    chunks, height, _ = gathered_ref.shape
    cols = out_ref.shape[1]
    per_chunk = LANES // cols
    chunk, slot = chip_index() // per_chunk, chip_index() % per_chunk
    want = lax.broadcasted_iota(jnp.int32, (cols, LANES), 0) + slot * cols
    have = lax.broadcasted_iota(jnp.int32, (cols, LANES), 1)
    pick = (want == have).astype(jnp.bfloat16)
    past = jnp.zeros((cols, out_ref.shape[2] - height), jnp.float32)

    def write(k, value):
        out_ref[k] = jnp.concatenate([value, past], axis=1) if past.shape[1] else value

    write(0, mm(pick, gathered_ref[chunk], NT))
    row = lax.broadcasted_iota(jnp.int32, (height, height), 0)
    col = lax.broadcasted_iota(jnp.int32, (height, height), 1)
    source = gathered_ref
    for step in range(ITERS):
        x = jnp.concatenate([source[q] for q in range(chunks)], axis=1)
        gram = mm(x, x, NT)
        if step == 0:
            norm = jnp.sqrt(jnp.sum(jnp.where(row == col, gram, 0.0), keepdims=True))
            scale = 1.0 / (norm + NORM_EPS)
            gram = gram * scale * scale
        gram = gram.astype(jnp.bfloat16)
        square = mm(gram, gram, NN)
        poly = (NEWTON_SECOND * gram.astype(jnp.float32) + NEWTON_THIRD * square).astype(jnp.bfloat16)
        if step == ITERS - 1:
            mine = mm(pick, x_ref[chunk], NT)
            write(1, NEWTON_FIRST * mine + mm(mine.astype(jnp.bfloat16), poly, NT))
            break
        for q in range(0, chunks, 2):
            part = jnp.concatenate([source[q], source[q + 1]], axis=1)
            part = NEWTON_FIRST * part.astype(jnp.float32) + mm(poly, part, NN)
            if step == 0:
                part = part * scale
            part = part.astype(jnp.bfloat16)
            x_ref[q] = part[:, :LANES]
            x_ref[q + 1] = part[:, LANES:]
        source = x_ref


def newton(gathered, cols, height):
    return pl.pallas_call(
        newton_kernel,
        in_specs=[VMEM],
        out_specs=VMEM,
        out_shape=jax.ShapeDtypeStruct((2, cols, height), jnp.float32),
        scratch_shapes=[pltpu.VMEM(gathered.shape, jnp.bfloat16)],
        compiler_params=PARAMS,
    )(gathered)


def finish_kernel(factor, back_ref, weights_ref, new_ref, update_ref):
    mats, slab, _ = weights_ref.shape
    mine = pl.ds(pl.multiple_of(lax.axis_index("core") * slab, slab), slab)
    for m in range(mats):
        new_ref[m] = back_ref[m, 0, mine, :]
        update_ref[m] = factor * back_ref[m, 1, mine, :] + WEIGHT_DECAY * weights_ref[m]


def finish(back, weights, factor):
    def kernel(*refs):
        finish_kernel(factor, *refs)

    shape = jax.ShapeDtypeStruct(weights.shape, jnp.float32)
    return pl.pallas_call(
        kernel,
        in_specs=[VMEM, VMEM],
        out_specs=[VMEM, VMEM],
        out_shape=[shape, shape],
        compiler_params=PARAMS,
    )(back, weights)


def per_device(grads, momentum, weights, live_rows):
    mats, height, slab = momentum.shape
    cores = lax.axis_size("core")
    width = grads.shape[3]
    core = lax.axis_index("core")
    group = ("y_low", "x")
    old = jnp.swapaxes(momentum, 1, 2)
    other = lax.ppermute(take_other(grads[0], old), "core", [(0, 1), (1, 0)])
    def chain(rows):
        chunks = pair_sum(grads[0], other, old, rows)
        chunks = lax.all_to_all(chunks, group, 0, 0)
        chunk = sum_and_copy(chunks, lax.axis_size("y_high"))
        chunk = lax.all_to_all(chunk, "y_high", 0, 0)
        copies = sum_mask_and_copy(mats, live_rows, chunk, width // LANES)
        gathered = lax.all_to_all(copies, group, 0, 0)
        return newton(gathered, cores * slab, height)

    live = lax.dynamic_index_in_dim(live_rows, lax.axis_index("own") * mats + core, 0, keepdims=False)
    step, least = 32, 192
    counts = range(least, height + 1, step)
    level = jnp.maximum(live - least + step - 1, 0) // step
    mine = lax.switch(level, [functools.partial(chain, rows) for rows in counts])
    back = lax.all_gather(mine, "core")
    new_momentum, update = finish(
        back, jnp.swapaxes(weights, 1, 2), UPDATE_SCALE * math.sqrt(width)
    )
    return (jnp.swapaxes(new_momentum, 1, 2), jnp.swapaxes(update, 1, 2))


def solution(mesh):
    fsdp, own = mesh.devices.shape
    assert (fsdp, own) == (64, 12)
    split = Mesh(mesh.devices.reshape(4, 4, 2, 2, own), ("x", "y_high", "y_low", "core", "own"))
    all_fsdp = ("x", "y_high", "y_low", "core")
    in_specs = (P(all_fsdp, "own", None, None), P("own", None, all_fsdp), P("own", None, all_fsdp), P())
    out_specs = (P("own", None, all_fsdp), P("own", None, all_fsdp))
    return jax.shard_map(
        per_device, mesh=split, in_specs=in_specs, out_specs=out_specs, check_vma=False
    )
```
